32 devices in a mesh: ctx: 8 (over y, x, core), head: 4 (over z).
Axes of the slice: x: 2, y: 2, z: 4, core: 2. Of those that a mesh axis runs over, the one named last changes fastest.
Arguments:
- queries: bfloat16 [1024, 64, 576], P('ctx', 'head'), may hold values from -64 to 64
- latents: bfloat16 [1024, 576], P('ctx'), may hold values from -6 to 6
- grad_out: bfloat16 [1024, 64, 512], P('ctx', 'head'), may hold values from -6 to 6
- block_order: int32 [8], replicated, may hold values from 0 to 7, each once
- doc_ids: int32 [1024], replicated, may hold values from 0 to 3, never falling along the last dimension, each value on 1 to 512 neighbouring positions
Outputs:
- out_lat: bfloat16 [1024, 64, 512], P('ctx', 'head')
- grad_queries: bfloat16 [1024, 64, 576], P('ctx', 'head')
- grad_latents: float32 [1024, 576], P('ctx')
The draws below stay inside these ranges and needn't reach their ends.
Inputs may be any that keep to these rules, and one draw needn't show every extreme that they name: Each number appears once; shard i of the token dimension holds the 64 positions of block block_order[i] followed by those of block 15 - block_order[i]. `doc_ids`: never falling along positions; every document holds 1 to 512 positions and one holds exactly 512.
All inputs are finite; a program needn't handle non-finite values.
Results may differ from the reference program's by a relative error of at most 0.014.
Values may be sent and summed in bfloat16 or wider, within the bound.
A program may use at most 128 MiB of HBM per device.

```python
import math
import jax
import jax.numpy as jnp
import numpy as np
from jax import lax

LAT = 512
ROPE = 64
HEADS = 64
TOK_DEV = 128
DOCS = 4
HALF = 64
SEQ = 1024
LONGEST = 512
N_CTX = 8


def latent_base(key):
    base_rows = jax.random.normal(jax.random.fold_in(key, 7), (SEQ, LAT + ROPE), jnp.float32)
    return jnp.clip(base_rows, -5.5, 5.5)


def draw_latents(key, part):
    base_rows = latent_base(key)
    return base_rows.astype(jnp.bfloat16)


def draw_queries(key, part):
    key = jax.random.fold_in(key, 2)
    values = jnp.clip(jax.random.normal(key, (SEQ, HEADS, LAT + ROPE), jnp.float32), -5.5, 5.5)
    return values.astype(jnp.bfloat16)


def level_of(rng, dims, split, least, top_value):
    def one(axis_at, parts):
        heights = jax.random.uniform(jax.random.fold_in(jax.random.fold_in(rng, 6), axis_at), (parts,), jnp.float32, least / len(split), top_value / len(split))
        return jnp.repeat(jnp.exp(heights), dims[axis_at] // parts).reshape((-1,) + (1,) * (len(dims) - axis_at - 1))

    gain = one(*split[0])
    for cut in split[1:]:
        gain = gain * one(*cut)
    return gain


def profile(number_of, total, bound, skew):
    portions = [(1 << 20) // math.isqrt(grade ** skew) + 1 for grade in range(2, number_of + 1)]
    surplus, given = total - bound - (number_of - 1), [1] * (number_of - 1)
    while surplus > 0:
        candidates = [i for i in range(number_of - 1) if given[i] < bound]
        pool, budget = sum([portions[i] for i in candidates]), surplus
        for i in candidates:
            more = min(bound - given[i], max(1, budget * portions[i] // pool), surplus)
            given[i] = given[i] + more
            surplus = surplus - more
    return np.array([bound] + given)


def uneven(stream_key, number_of, total, most, lean):
    if number_of == 2:
        one = jax.random.randint(stream_key, (), max(1, total - most), min(most, total - 1) + 1)
        return jnp.stack([one, total - one])
    sizes = jnp.asarray(profile(number_of, total, most, lean), jnp.int32)
    twos = (number_of - 1) // 2
    source_of, taker = sizes[1:1 + 2 * twos:2], sizes[2:2 + 2 * twos:2]
    room = jnp.minimum(source_of - 1, most - taker)
    passed = jax.random.randint(jax.random.fold_in(stream_key, 1), (twos,), 0, 1 << 20) % (room + 1)
    sizes = sizes.at[1:1 + 2 * twos:2].set(source_of - passed).at[2:2 + 2 * twos:2].set(taker + passed)
    return sizes[jax.random.permutation(jax.random.fold_in(stream_key, 2), number_of)]


def bell_draw(stream_key, dims, scale, bound, cuts=(), kind=jnp.bfloat16):
    array = scale * jax.random.normal(stream_key, dims, jnp.float32)
    if cuts:
        array = array * level_of(stream_key, dims, cuts, -0.22, 0.18)
    return jnp.clip(array, -bound, bound).astype(kind)


def setup_inputs(seed: int = 0) -> dict:
    seeds = jax.random.split(jax.random.key(seed), 6)
    return {
        "queries": draw_queries(jax.random.fold_in(seeds[5], 71), 0),
        "latents": draw_latents(jax.random.fold_in(seeds[5], 71), 0),
        "grad_out": bell_draw(seeds[2], (SEQ, HEADS, LAT), 1.0, 6.0, ((0, 8), (1, 4))),
        "block_order": jax.random.permutation(seeds[3], N_CTX).astype(jnp.int32),
        "doc_ids": jnp.searchsorted(jnp.cumsum(uneven(seeds[4], DOCS, SEQ, LONGEST, 0)), jnp.arange(SEQ), side="right").astype(jnp.int32),
    }


score_scale = 192.0 ** -0.5


def token_layout(block_order, doc_ids):
    row_ids = jnp.arange(SEQ, dtype=jnp.int32)
    owner_dev = row_ids // TOK_DEV
    within = row_ids % TOK_DEV
    low_block = jnp.take(block_order, owner_dev)
    block_ids = jnp.where(within < HALF, low_block, 2 * N_CTX - 1 - low_block)
    positions = (block_ids * HALF + within % HALF).astype(jnp.int32)
    return positions, jnp.take(doc_ids, positions)


def reference(queries, latents, grad_out, block_order, doc_ids):
    positions, docs = token_layout(block_order, doc_ids)
    visible = (positions[None, :] <= positions[:, None]) & (docs[None, :] == docs[:, None])
    values = latents[:, :LAT]

    def per_head(grad_lat, inputs):
        query_head, grad_head = inputs
        scores = jnp.dot(query_head, latents.T, preferred_element_type=jnp.float32) * score_scale
        scores = jnp.where(visible, scores, -jnp.inf)
        row_max = jnp.max(scores, axis=1, keepdims=True)
        expo_terms = jnp.exp(scores - row_max)
        row_sum = jnp.sum(expo_terms, axis=1, keepdims=True)
        weights = expo_terms.astype(jnp.bfloat16)
        out_head = (jnp.dot(weights, values, preferred_element_type=jnp.float32) / row_sum).astype(jnp.bfloat16)
        log_sum = row_max + jnp.log(row_sum)
        row_probs = jnp.exp(scores - log_sum)
        row_delta = jnp.sum(grad_head.astype(jnp.float32) * out_head.astype(jnp.float32), axis=1, keepdims=True)
        grad_probs = jnp.dot(grad_head, values.T, preferred_element_type=jnp.float32)
        grad_scores = (row_probs * (grad_probs - row_delta) * score_scale).astype(jnp.bfloat16)
        grad_query = jnp.dot(grad_scores, latents, preferred_element_type=jnp.float32).astype(jnp.bfloat16)
        key_term = jnp.dot(grad_scores.T, query_head, preferred_element_type=jnp.float32)
        value_term = jnp.dot(row_probs.astype(jnp.bfloat16).T, grad_head, preferred_element_type=jnp.float32)
        key_term = key_term.at[:, :LAT].add(value_term)
        return grad_lat + key_term, (out_head, grad_query)

    start_grad = jnp.zeros((SEQ, LAT + ROPE), jnp.float32)
    grad_latents, (out_heads, grad_heads) = lax.scan(
        per_head, start_grad, (jnp.swapaxes(queries, 0, 1), jnp.swapaxes(grad_out, 0, 1)))
    return jnp.swapaxes(out_heads, 0, 1), jnp.swapaxes(grad_heads, 0, 1), grad_latents
```

```python
import functools

import jax
import jax.numpy as jnp
from jax import lax
from jax.experimental import pallas as pl
from jax.experimental.pallas import tpu as pltpu
from jax.sharding import PartitionSpec as P

score_scale = 192.0 ** (-0.5)
far_below = -1e30
DOCS = 4
KEY_TILE = 256
ROWS = 512
NT = (((1,), (1,)), ((), ()))
NN = (((1,), (0,)), ((), ()))
TN = (((0,), (0,)), ((), ()))


def dot(a, b, dims):
    return lax.dot_general(a, b, dims, preferred_element_type=jnp.float32)


def attention_kernel(
    shape, order_ref, docs_ref, q_ref, g_ref, lat_ref, out_ref, gq_ref, gl_ref,
    keys, grad_keys, scores, acc, acc_q, bounds, sems,
):
    n_ctx, half, heads, chunk_tok, lat = shape
    seq = 2 * half * n_ctx
    c = pl.program_id(0)
    me = lax.axis_index("ctx")

    def block_of(slot):
        low = order_ref[slot // 2]
        return low if slot % 2 == 0 else 2 * n_ctx - 1 - low

    @pl.when(c == 0)
    def _():
        copies = []
        for slot in range(2 * n_ctx):
            first = pl.multiple_of(block_of(slot) * half, half)
            copy = pltpu.make_async_copy(
                lat_ref.at[pl.ds(slot * half, half)], keys.at[pl.ds(first, half)], sems.at[slot]
            )
            copy.start()
            copies.append(copy)
        keys[pl.ds(seq, KEY_TILE)] = jnp.zeros((KEY_TILE, keys.shape[1]), keys.dtype)
        grad_keys[...] = jnp.zeros_like(grad_keys)
        bounds[0] = 0
        for number in range(1, DOCS):
            at = jnp.int32(0)
            step = seq // 2
            while step >= 1:
                at = jnp.where(docs_ref[at + step - 1] < number, at + step, at)
                step //= 2
            bounds[number] = at
        for copy in copies:
            copy.wait()

    low = order_ref[me]
    first_tok = c * chunk_tok
    block = jnp.where(first_tok < half, low, 2 * n_ctx - 1 - low)
    pos0 = block * half + lax.rem(first_tok, half)
    doc_start = jnp.int32(0)
    for number in range(1, DOCS):
        doc_start = jnp.where(bounds[number] <= pos0, bounds[number], doc_start)
    start = (doc_start // 16) * 16
    tiles = (pos0 + chunk_tok - start + KEY_TILE - 1) // KEY_TILE

    rows = chunk_tok * heads
    row_pos = pos0 + lax.broadcasted_iota(jnp.int32, (rows, 1), 0) // heads
    row_doc = jnp.zeros_like(row_pos)
    for number in range(1, DOCS):
        row_doc = jnp.where(bounds[number] <= row_pos, bounds[number], row_doc)
    q = q_ref[...]
    g = g_ref[...]

    def tile_at(i):
        return pl.ds(pl.multiple_of(start + i * KEY_TILE, 16), KEY_TILE)

    def first_pass(i, row_max):
        s = dot(q, keys[tile_at(i), :], NT) * score_scale
        key_pos = start + i * KEY_TILE + lax.broadcasted_iota(jnp.int32, (1, KEY_TILE), 1)
        s = jnp.where((key_pos <= row_pos) & (key_pos >= row_doc), s, far_below)
        scores[i] = s
        return jnp.maximum(row_max, jnp.max(s, axis=1, keepdims=True))

    row_max = lax.fori_loop(0, tiles, first_pass, jnp.full((rows, 1), far_below, jnp.float32))
    acc[...] = jnp.zeros_like(acc)

    def second_pass(i, row_sum):
        e = jnp.exp(scores[i] - row_max)
        scores[i] = e
        acc[...] += dot(e.astype(jnp.bfloat16), keys[tile_at(i), :lat], NN)
        return row_sum + jnp.sum(e, axis=1, keepdims=True)

    row_sum = lax.fori_loop(0, tiles, second_pass, jnp.zeros((rows, 1), jnp.float32))
    inverse = 1.0 / row_sum
    out = (acc[...] * inverse).astype(jnp.bfloat16)
    out_ref[...] = out
    delta = jnp.sum(g.astype(jnp.float32) * out.astype(jnp.float32), axis=1, keepdims=True)
    acc_q[...] = jnp.zeros_like(acc_q)

    def third_pass(i, carry):
        at = tile_at(i)
        grad_probs = dot(g, keys[at, :lat], NT)
        probs = scores[i] * inverse
        ds = (probs * (grad_probs - delta) * score_scale).astype(jnp.bfloat16)
        acc_q[...] += dot(ds, keys[at, :], NN)
        grad_keys[at, :] += dot(ds, q, TN)
        grad_keys[at, :lat] += dot(probs.astype(jnp.bfloat16), g, TN)
        return carry

    lax.fori_loop(0, tiles, third_pass, 0)
    gq_ref[...] = acc_q[...].astype(jnp.bfloat16)

    @pl.when(c == pl.num_programs(0) - 1)
    def _():
        for slot in range(2 * n_ctx):
            first = pl.multiple_of(block_of(slot) * half, half)
            gl_ref[pl.ds(slot * half, half), :] = grad_keys[pl.ds(first, half), :].astype(
                gl_ref.dtype
            )


def attention(queries, grad_out, all_lat, block_order, doc_ids, n_ctx, sum_type):
    tok, heads, width = queries.shape
    lat = grad_out.shape[2]
    half = tok // 2
    seq = tok * n_ctx
    chunk_tok = min(half, max(1, ROWS // heads))
    rows = chunk_tok * heads
    tile_count = seq // KEY_TILE + 1
    block = lambda w: pl.BlockSpec((rows, w), lambda c, *_: (c, 0))
    out, gq, gl = pl.pallas_call(
        functools.partial(attention_kernel, (n_ctx, half, heads, chunk_tok, lat)),
        grid_spec=pltpu.PrefetchScalarGridSpec(
            num_scalar_prefetch=2,
            grid=(tok // chunk_tok,),
            in_specs=[block(width), block(lat), pl.BlockSpec(memory_space=pl.ANY)],
            out_specs=[
                block(lat),
                block(width),
                pl.BlockSpec((seq, width), lambda c, *_: (0, 0)),
            ],
            scratch_shapes=[
                pltpu.VMEM((seq + KEY_TILE, width), jnp.bfloat16),
                pltpu.VMEM((seq + KEY_TILE, width), jnp.float32),
                pltpu.VMEM((tile_count, rows, KEY_TILE), jnp.float32),
                pltpu.VMEM((rows, lat), jnp.float32),
                pltpu.VMEM((rows, width), jnp.float32),
                pltpu.SMEM((DOCS,), jnp.int32),
                pltpu.SemaphoreType.DMA((2 * n_ctx,)),
            ],
        ),
        out_shape=[
            jax.ShapeDtypeStruct((tok * heads, lat), jnp.bfloat16),
            jax.ShapeDtypeStruct((tok * heads, width), jnp.bfloat16),
            jax.ShapeDtypeStruct((seq, width), sum_type),
        ],
        compiler_params=pltpu.CompilerParams(vmem_limit_bytes=48 * 1024 * 1024),
        cost_estimate=pl.CostEstimate(
            flops=14 * tok * heads * seq * lat // 2, bytes_accessed=12 << 20, transcendentals=0
        ),
    )(
        block_order, doc_ids,
        queries.reshape(tok * heads, width), grad_out.reshape(tok * heads, lat), all_lat,
    )
    return out.reshape(tok, heads, lat), gq.reshape(tok, heads, width), gl


def body(queries, latents, grad_out, block_order, doc_ids):
    n_ctx = lax.axis_size("ctx")
    all_lat = lax.all_gather(latents, "ctx", axis=0, tiled=True)
    out, gq, gl = attention(queries, grad_out, all_lat, block_order, doc_ids, n_ctx, jnp.float32)
    own_rows = lax.psum_scatter(gl, "ctx", scatter_dimension=0, tiled=True)
    return out, gq, lax.psum(own_rows, "head")


def solution(mesh):
    return jax.shard_map(
        body,
        mesh=mesh,
        in_specs=(P("ctx", "head", None), P("ctx", None), P("ctx", "head", None), P(), P()),
        out_specs=(P("ctx", "head", None), P("ctx", "head", None), P("ctx", None)),
        check_vma=False,
    )
```

```python
import functools

import jax
import jax.numpy as jnp
from jax import lax
from jax.experimental import pallas as pl
from jax.experimental.pallas import tpu as pltpu
from jax.sharding import PartitionSpec as P

score_scale = 192.0 ** (-0.5)
far_below = -1e30
DOCS = 4
KEY_TILE = 256
ROWS = 512
NT = (((1,), (1,)), ((), ()))
NN = (((1,), (0,)), ((), ()))
TN = (((0,), (0,)), ((), ()))


def dot(a, b, dims):
    return lax.dot_general(a, b, dims, preferred_element_type=jnp.float32)


def attention_kernel(
    shape, order_ref, docs_ref, q_ref, g_ref, lat_ref, out_ref, gq_ref, gl_ref,
    keys, grad_keys, scores, acc, acc_q, bounds, sems,
):
    n_ctx, half, heads, chunk_tok, lat = shape
    seq = 2 * half * n_ctx
    c = pl.program_id(0)
    me = lax.axis_index("ctx")

    def block_of(slot):
        low = order_ref[slot // 2]
        return low if slot % 2 == 0 else 2 * n_ctx - 1 - low

    @pl.when(c == 0)
    def _():
        copies = []
        for slot in range(2 * n_ctx):
            first = pl.multiple_of(block_of(slot) * half, half)
            copy = pltpu.make_async_copy(
                lat_ref.at[pl.ds(slot * half, half)], keys.at[pl.ds(first, half)], sems.at[slot]
            )
            copy.start()
            copies.append(copy)
        keys[pl.ds(seq, KEY_TILE)] = jnp.zeros((KEY_TILE, keys.shape[1]), keys.dtype)
        grad_keys[...] = jnp.zeros_like(grad_keys)
        bounds[0] = 0
        for number in range(1, DOCS):
            at = jnp.int32(0)
            step = seq // 2
            while step >= 1:
                at = jnp.where(docs_ref[at + step - 1] < number, at + step, at)
                step //= 2
            bounds[number] = at
        for copy in copies:
            copy.wait()

    low = order_ref[me]
    first_tok = c * chunk_tok
    block = jnp.where(first_tok < half, low, 2 * n_ctx - 1 - low)
    pos0 = block * half + lax.rem(first_tok, half)
    doc_start = jnp.int32(0)
    for number in range(1, DOCS):
        doc_start = jnp.where(bounds[number] <= pos0, bounds[number], doc_start)
    start = (doc_start // 16) * 16
    tiles = (pos0 + chunk_tok - start + KEY_TILE - 1) // KEY_TILE

    rows = chunk_tok * heads
    row_pos = pos0 + lax.broadcasted_iota(jnp.int32, (rows, 1), 0) // heads
    row_doc = jnp.zeros_like(row_pos)
    for number in range(1, DOCS):
        row_doc = jnp.where(bounds[number] <= row_pos, bounds[number], row_doc)
    q = q_ref[...]
    g = g_ref[...]

    def tile_at(i):
        return pl.ds(pl.multiple_of(start + i * KEY_TILE, 16), KEY_TILE)

    def first_pass(i, row_max):
        s = dot(q, keys[tile_at(i), :], NT) * score_scale
        key_pos = start + i * KEY_TILE + lax.broadcasted_iota(jnp.int32, (1, KEY_TILE), 1)
        s = jnp.where((key_pos <= row_pos) & (key_pos >= row_doc), s, far_below)
        scores[i] = s
        return jnp.maximum(row_max, jnp.max(s, axis=1, keepdims=True))

    row_max = lax.fori_loop(0, tiles, first_pass, jnp.full((rows, 1), far_below, jnp.float32))
    acc[...] = jnp.zeros_like(acc)

    def second_pass(i, row_sum):
        e = jnp.exp(scores[i] - row_max)
        scores[i] = e
        acc[...] += dot(e.astype(jnp.bfloat16), keys[tile_at(i), :lat], NN)
        return row_sum + jnp.sum(e, axis=1, keepdims=True)

    row_sum = lax.fori_loop(0, tiles, second_pass, jnp.zeros((rows, 1), jnp.float32))
    inverse = 1.0 / row_sum
    out = (acc[...] * inverse).astype(jnp.bfloat16)
    out_ref[...] = out
    delta = jnp.sum(g.astype(jnp.float32) * out.astype(jnp.float32), axis=1, keepdims=True)
    acc_q[...] = jnp.zeros_like(acc_q)

    def third_pass(i, carry):
        at = tile_at(i)
        grad_probs = dot(g, keys[at, :lat], NT)
        probs = scores[i] * inverse
        ds = (probs * (grad_probs - delta) * score_scale).astype(jnp.bfloat16)
        acc_q[...] += dot(ds, keys[at, :], NN)
        grad_keys[at, :] += dot(ds, q, TN)
        grad_keys[at, :lat] += dot(probs.astype(jnp.bfloat16), g, TN)
        return carry

    lax.fori_loop(0, tiles, third_pass, 0)
    gq_ref[...] = acc_q[...].astype(jnp.bfloat16)

    @pl.when(c == pl.num_programs(0) - 1)
    def _():
        for slot in range(2 * n_ctx):
            first = pl.multiple_of(block_of(slot) * half, half)
            gl_ref[pl.ds(slot * half, half), :] = grad_keys[pl.ds(first, half), :].astype(
                gl_ref.dtype
            )


def attention(queries, grad_out, all_lat, block_order, doc_ids, n_ctx, sum_type):
    tok, heads, width = queries.shape
    lat = grad_out.shape[2]
    half = tok // 2
    seq = tok * n_ctx
    chunk_tok = min(half, max(1, ROWS // heads))
    rows = chunk_tok * heads
    tile_count = seq // KEY_TILE + 1
    block = lambda w: pl.BlockSpec((rows, w), lambda c, *_: (c, 0))
    out, gq, gl = pl.pallas_call(
        functools.partial(attention_kernel, (n_ctx, half, heads, chunk_tok, lat)),
        grid_spec=pltpu.PrefetchScalarGridSpec(
            num_scalar_prefetch=2,
            grid=(tok // chunk_tok,),
            in_specs=[block(width), block(lat), pl.BlockSpec(memory_space=pl.ANY)],
            out_specs=[
                block(lat),
                block(width),
                pl.BlockSpec((seq, width), lambda c, *_: (0, 0)),
            ],
            scratch_shapes=[
                pltpu.VMEM((seq + KEY_TILE, width), jnp.bfloat16),
                pltpu.VMEM((seq + KEY_TILE, width), jnp.float32),
                pltpu.VMEM((tile_count, rows, KEY_TILE), jnp.float32),
                pltpu.VMEM((rows, lat), jnp.float32),
                pltpu.VMEM((rows, width), jnp.float32),
                pltpu.SMEM((DOCS,), jnp.int32),
                pltpu.SemaphoreType.DMA((2 * n_ctx,)),
            ],
        ),
        out_shape=[
            jax.ShapeDtypeStruct((tok * heads, lat), jnp.bfloat16),
            jax.ShapeDtypeStruct((tok * heads, width), jnp.bfloat16),
            jax.ShapeDtypeStruct((seq, width), sum_type),
        ],
        compiler_params=pltpu.CompilerParams(vmem_limit_bytes=48 * 1024 * 1024),
        cost_estimate=pl.CostEstimate(
            flops=14 * tok * heads * seq * lat // 2, bytes_accessed=12 << 20, transcendentals=0
        ),
    )(
        block_order, doc_ids,
        queries.reshape(tok * heads, width), grad_out.reshape(tok * heads, lat), all_lat,
    )
    return out.reshape(tok, heads, lat), gq.reshape(tok, heads, width), gl


def transfer(src, dst, sems, index, device):
    copy = pltpu.make_async_remote_copy(
        src_ref=src, dst_ref=dst, send_sem=sems.at[0, index], recv_sem=sems.at[1, index],
        device_id=device, device_id_type=pl.DeviceIdType.MESH,
    )
    copy.start()
    return copy


def greet(peers):
    barrier = pltpu.get_barrier_semaphore()
    for peer in peers:
        pl.semaphore_signal(
            barrier, inc=1, device_id=peer, device_id_type=pl.DeviceIdType.MESH
        )
    pl.semaphore_wait(barrier, len(peers))


def places(n_ctx):
    me = lax.axis_index("ctx")
    core = lax.rem(me, 2)
    chip = me // 2
    sibling = chip * 2 + 1 - core
    chips = n_ctx // 2
    return me, core, chip, sibling, chips


def gather_kernel(n_ctx, lat_ref, out_ref, own, sems, pair_sems, local_sem):
    me, core, chip, sibling, chips = places(n_ctx)
    z = lax.axis_index("head")
    others = [lax.rem(chip + k, chips) * 2 + core for k in range(1, chips)]
    greet([(sibling, z)] + [(other, z) for other in others])
    own[...] = lat_ref[...].T
    sends = [
        transfer(own, out_ref.at[me], sems, k, (other, z)) for k, other in enumerate(others)
    ]
    pairs = [transfer(own, out_ref.at[me], pair_sems, 0, (sibling, z))]
    keep = pltpu.make_async_copy(own, out_ref.at[me], local_sem)
    keep.start()
    for k in range(1, chips):
        sends[k - 1].wait_recv()
        owner = lax.rem(chip + chips - k, chips) * 2 + core
        pairs.append(
            transfer(out_ref.at[owner], out_ref.at[owner], pair_sems, k, (sibling, z))
        )
    for copy in sends:
        copy.wait_send()
    for copy in pairs:
        copy.wait()
    keep.wait()


def gather(latents, n_ctx):
    tok, width = latents.shape
    out = pl.pallas_call(
        functools.partial(gather_kernel, n_ctx),
        in_specs=[pl.BlockSpec(memory_space=pltpu.VMEM)],
        out_specs=pl.BlockSpec(memory_space=pl.ANY),
        out_shape=jax.ShapeDtypeStruct((n_ctx, tok, width), latents.dtype),
        scratch_shapes=[
            pltpu.VMEM((tok, width), latents.dtype),
            pltpu.SemaphoreType.DMA((2, n_ctx // 2)),
            pltpu.SemaphoreType.DMA((2, n_ctx // 2)),
            pltpu.SemaphoreType.DMA,
        ],
        compiler_params=pltpu.CompilerParams(collective_id=0, has_side_effects=True),
    )(latents.T)
    return out.reshape(n_ctx * tok, width)


def reduce_kernel(
    n_ctx, n_head, part_ref, out_ref, pair_in, chip_out, chip_in, head_out, head_in, whole,
    pair_sems, chip_sems, head_sems, last_sems,
):
    me, core, chip, sibling, chips = places(n_ctx)
    z = lax.axis_index("head")
    others = [lax.rem(chip + k, chips) * 2 + core for k in range(1, chips)]
    heads = [lax.rem(z + k, n_head) for k in range(1, n_head)]
    greet(
        [(sibling, z)] + [(other, z) for other in others] + [(me, other) for other in heads]
    )
    order = [lax.rem(chip + k, chips) for k in range(1, chips + 1)]
    pairs = [
        transfer(
            part_ref.at[target * 2 + 1 - core], pair_in.at[k], pair_sems, k, (sibling, z)
        )
        for k, target in enumerate(order)
    ]
    sends = []
    total = None
    for k, target in enumerate(order):
        pairs[k].wait_recv()
        total = part_ref[target * 2 + core].astype(jnp.float32) + pair_in[k].astype(jnp.float32)
        if k < chips - 1:
            chip_out[k] = total.astype(jnp.bfloat16)
            sends.append(
                transfer(chip_out.at[k], chip_in.at[k], chip_sems, k, (others[k], z))
            )
    for k, copy in enumerate(sends):
        copy.wait_recv()
        total = total + chip_in[k].astype(jnp.float32)
    rows = total.shape[0] // n_head
    for k in range(n_head):
        head_out[k] = total[k * rows : (k + 1) * rows].astype(jnp.bfloat16)
    steps = [
        transfer(head_out.at[other], head_in.at[k], head_sems, k, (me, other))
        for k, other in enumerate(heads)
    ]
    piece = head_out[z].astype(jnp.float32)
    for k, copy in enumerate(steps):
        copy.wait_recv()
        piece = piece + head_in[k].astype(jnp.float32)
    whole[z] = piece.astype(jnp.bfloat16)
    lasts = [
        transfer(whole.at[z], whole.at[z], last_sems, k, (me, other))
        for k, other in enumerate(heads)
    ]
    for copy in lasts:
        copy.wait_recv()
    result = jnp.concatenate([whole[k] for k in range(n_head)], axis=0)
    out_ref[...] = result.astype(jnp.float32).T
    for copy in pairs + sends + steps + lasts:
        copy.wait_send()


def reduce_parts(parts, n_ctx, n_head):
    seq, width = parts.shape
    tok = seq // n_ctx
    rows = tok // n_head
    chips = n_ctx // 2
    kind = parts.dtype
    vmem = pl.BlockSpec(memory_space=pltpu.VMEM)
    out = pl.pallas_call(
        functools.partial(reduce_kernel, n_ctx, n_head),
        in_specs=[vmem],
        out_specs=vmem,
        out_shape=jax.ShapeDtypeStruct((width, tok), jnp.float32),
        scratch_shapes=[
            pltpu.VMEM((chips, tok, width), kind),
            pltpu.VMEM((chips, tok, width), kind),
            pltpu.VMEM((chips, tok, width), kind),
            pltpu.VMEM((n_head, rows, width), kind),
            pltpu.VMEM((n_head, rows, width), kind),
            pltpu.VMEM((n_head, rows, width), kind),
            pltpu.SemaphoreType.DMA((2, chips)),
            pltpu.SemaphoreType.DMA((2, chips)),
            pltpu.SemaphoreType.DMA((2, n_head)),
            pltpu.SemaphoreType.DMA((2, n_head)),
        ],
        compiler_params=pltpu.CompilerParams(
            collective_id=1, has_side_effects=True, vmem_limit_bytes=32 * 1024 * 1024
        ),
    )(parts.reshape(n_ctx, tok, width))
    return out.T


def body(queries, latents, grad_out, block_order, doc_ids):
    n_ctx = lax.axis_size("ctx")
    n_head = lax.axis_size("head")
    all_lat = gather(latents, n_ctx)
    out, gq, gl = attention(queries, grad_out, all_lat, block_order, doc_ids, n_ctx, jnp.bfloat16)
    return out, gq, reduce_parts(gl, n_ctx, n_head)


def solution(mesh):
    return jax.shard_map(
        body,
        mesh=mesh,
        in_specs=(P("ctx", "head", None), P("ctx", None), P("ctx", "head", None), P(), P()),
        out_specs=(P("ctx", "head", None), P("ctx", "head", None), P("ctx", None)),
        check_vma=False,
    )
```

```python
import functools

import jax
import jax.numpy as jnp
from jax import lax
from jax.experimental import pallas as pl
from jax.experimental.pallas import tpu as pltpu
from jax.sharding import PartitionSpec as P

score_scale = 192.0 ** (-0.5)
far_below = -1e30
DOCS = 4
KEY_TILE = 256
COLS = 512
LANES = 128
NT = (((1,), (1,)), ((), ()))
NN = (((1,), (0,)), ((), ()))
TN = (((0,), (0,)), ((), ()))


def dot(a, b, dims):
    return lax.dot_general(a, b, dims, preferred_element_type=jnp.float32)


def attention_kernel(
    shape, order_ref, docs_ref, q_ref, g_ref, lat_ref, out_ref, gq_ref, gl_ref,
    keys, grad_keys, scores, grad_probs, out_acc, q_acc, by_token, bounds, sems,
):
    n_ctx, half, heads, cols, lat = shape
    seq = 2 * half * n_ctx
    part = pl.program_id(0)
    me = lax.axis_index("ctx")

    def block_of(slot):
        low = order_ref[slot // 2]
        return low if slot % 2 == 0 else 2 * n_ctx - 1 - low

    @pl.when(part == 0)
    def _():
        copies = []
        for slot in range(2 * n_ctx):
            first = pl.multiple_of(block_of(slot) * half, half)
            copy = pltpu.make_async_copy(
                lat_ref.at[pl.ds(slot * half, half)], keys.at[pl.ds(first, half)], sems.at[slot]
            )
            copy.start()
            copies.append(copy)
        keys[pl.ds(seq, KEY_TILE)] = jnp.zeros((KEY_TILE, keys.shape[1]), keys.dtype)
        grad_keys[...] = jnp.zeros_like(grad_keys)
        bounds[0] = 0
        for number in range(1, DOCS):
            at = jnp.int32(0)
            step = seq // 2
            while step >= 1:
                at = jnp.where(docs_ref[at + step - 1] < number, at + step, at)
                step //= 2
            bounds[number] = at
        for copy in copies:
            copy.wait()

    low = order_ref[me]
    pos0 = jnp.where(part == 0, low, 2 * n_ctx - 1 - low) * half
    doc_start = jnp.int32(0)
    for number in range(1, DOCS):
        doc_start = jnp.where(bounds[number] <= pos0, bounds[number], doc_start)
    start = (doc_start // 16) * 16
    tiles = (pos0 + half - start + KEY_TILE - 1) // KEY_TILE

    row_pos = pos0 + lax.rem(lax.broadcasted_iota(jnp.int32, (1, cols), 1), half)
    row_doc = jnp.zeros_like(row_pos)
    for number in range(1, DOCS):
        row_doc = jnp.where(bounds[number] <= row_pos, bounds[number], row_doc)

    def tile_at(i):
        return pl.ds(pl.multiple_of(start + i * KEY_TILE, 16), KEY_TILE)

    heads_now = cols // half
    for chunk in range(heads * half // cols):
        here = slice(chunk * cols, (chunk + 1) * cols)

        def first_pass(i, row_max):
            at = tile_at(i)
            s = dot(keys[at, :], q_ref[0, :, here], NN) * score_scale
            key_pos = start + i * KEY_TILE + lax.broadcasted_iota(jnp.int32, (KEY_TILE, 1), 0)
            s = jnp.where((key_pos <= row_pos) & (key_pos >= row_doc), s, far_below)
            scores[i] = s
            grad_probs[i] = dot(keys[at, :lat], g_ref[0, here, :], NT)
            return jnp.maximum(row_max, jnp.max(s, axis=0, keepdims=True))

        row_max = lax.fori_loop(
            0, tiles, first_pass, jnp.full((1, cols), far_below, jnp.float32)
        )

        def second_pass(i, sums):
            row_sum, weighted = sums
            e = jnp.exp(scores[i] - row_max)
            scores[i] = e
            return (
                row_sum + jnp.sum(e, axis=0, keepdims=True),
                weighted + jnp.sum(e * grad_probs[i], axis=0, keepdims=True),
            )

        zero = jnp.zeros((1, cols), jnp.float32)
        row_sum, weighted = lax.fori_loop(0, tiles, second_pass, (zero, zero))
        inverse = 1.0 / row_sum
        delta = weighted * inverse
        scaled = inverse * score_scale
        out_acc[...] = jnp.zeros_like(out_acc)
        q_acc[...] = jnp.zeros_like(q_acc)

        def third_pass(i, carry):
            at = tile_at(i)
            e = scores[i]
            probs = (e * inverse).astype(jnp.bfloat16)
            ds = (e * scaled * (grad_probs[i] - delta)).astype(jnp.bfloat16)
            out_acc[...] += dot(probs, keys[at, :lat], TN)
            q_acc[...] += dot(keys[at, :], ds, TN)
            key_term = dot(ds, q_ref[0, :, here], NT)
            value_term = dot(probs, g_ref[0, here, :], NN)
            grad_keys[at, :lat] += key_term[:, :lat] + value_term
            grad_keys[at, lat:] += key_term[:, lat:]
            return carry

        lax.fori_loop(0, tiles, third_pass, 0)
        for k in range(heads_now):
            head = chunk * heads_now + k
            mine = slice(k * half, (k + 1) * half)
            for lanes in range(lat // LANES):
                by_token[lanes, pl.ds(head, half, stride=heads), :] = out_acc[
                    mine, lanes * LANES : (lanes + 1) * LANES
                ]

        for p in range(2):
            @pl.when(part == p)
            def _():
                for k in range(heads_now):
                    head = chunk * heads_now + k
                    mine = slice(k * half, (k + 1) * half)
                    gq_ref[head, :, p * half : (p + 1) * half] = q_acc[:, mine].astype(
                        gq_ref.dtype
                    )

    for lanes in range(lat // LANES):
        out_ref[:, lanes * LANES : (lanes + 1) * LANES] = by_token[lanes].astype(out_ref.dtype)

    @pl.when(part == 1)
    def _():
        for slot in range(2 * n_ctx):
            first = pl.multiple_of(block_of(slot) * half, half)
            gl_ref[pl.ds(slot * half, half), :] = grad_keys[pl.ds(first, half), :].astype(
                gl_ref.dtype
            )


def attention(q_cols, g_rows, all_lat, block_order, doc_ids, n_ctx, heads):
    width, total = q_cols.shape[1:]
    lat = g_rows.shape[2]
    half = total // heads
    tok = 2 * half
    seq = tok * n_ctx
    cols = min(total, COLS)
    tile_count = seq // KEY_TILE + 1
    return pl.pallas_call(
        functools.partial(attention_kernel, (n_ctx, half, heads, cols, lat)),
        grid_spec=pltpu.PrefetchScalarGridSpec(
            num_scalar_prefetch=2,
            grid=(2,),
            in_specs=[
                pl.BlockSpec((1, width, total), lambda p, *_: (p, 0, 0)),
                pl.BlockSpec((1, total, lat), lambda p, *_: (p, 0, 0)),
                pl.BlockSpec(memory_space=pl.ANY),
            ],
            out_specs=[
                pl.BlockSpec((total, lat), lambda p, *_: (p, 0)),
                pl.BlockSpec((heads, width, tok), lambda p, *_: (0, 0, 0)),
                pl.BlockSpec((seq, width), lambda p, *_: (0, 0)),
            ],
            scratch_shapes=[
                pltpu.VMEM((seq + KEY_TILE, width), jnp.bfloat16),
                pltpu.VMEM((seq + KEY_TILE, width), jnp.float32),
                pltpu.VMEM((tile_count, KEY_TILE, cols), jnp.float32),
                pltpu.VMEM((tile_count, KEY_TILE, cols), jnp.float32),
                pltpu.VMEM((cols, lat), jnp.float32),
                pltpu.VMEM((width, cols), jnp.float32),
                pltpu.VMEM((lat // LANES, total, LANES), jnp.float32),
                pltpu.SMEM((DOCS,), jnp.int32),
                pltpu.SemaphoreType.DMA((2 * n_ctx,)),
            ],
        ),
        out_shape=[
            jax.ShapeDtypeStruct((tok * heads, lat), jnp.bfloat16),
            jax.ShapeDtypeStruct((heads, width, tok), jnp.bfloat16),
            jax.ShapeDtypeStruct((seq, width), jnp.bfloat16),
        ],
        compiler_params=pltpu.CompilerParams(vmem_limit_bytes=48 * 1024 * 1024),
        cost_estimate=pl.CostEstimate(
            flops=14 * tok * heads * seq * lat // 2, bytes_accessed=12 << 20, transcendentals=0
        ),
    )(block_order, doc_ids, q_cols, g_rows, all_lat)


def transfer(src, dst, sems, index, device):
    copy = pltpu.make_async_remote_copy(
        src_ref=src, dst_ref=dst, send_sem=sems.at[0, index], recv_sem=sems.at[1, index],
        device_id=device, device_id_type=pl.DeviceIdType.MESH,
    )
    copy.start()
    return copy


def greet(peers):
    barrier = pltpu.get_barrier_semaphore()
    for peer in peers:
        pl.semaphore_signal(
            barrier, inc=1, device_id=peer, device_id_type=pl.DeviceIdType.MESH
        )
    pl.semaphore_wait(barrier, len(peers))


def places(n_ctx):
    me = lax.axis_index("ctx")
    core = lax.rem(me, 2)
    chip = me // 2
    sibling = chip * 2 + 1 - core
    chips = n_ctx // 2
    return me, core, chip, sibling, chips


def gather_kernel(
    n_ctx, lat_ref, q_hbm, g_hbm, out_ref, q_out, g_out, own, q_in, g_in, g_wide,
    sems, pair_sems, local_sems,
):
    me, core, chip, sibling, chips = places(n_ctx)
    z = lax.axis_index("head")
    others = [lax.rem(chip + k, chips) * 2 + core for k in range(1, chips)]
    loads = [
        pltpu.make_async_copy(q_hbm, q_in, local_sems.at[0]),
        pltpu.make_async_copy(g_hbm, g_in, local_sems.at[1]),
    ]
    for load in loads:
        load.start()
    own[...] = lat_ref[...].T
    greet([(sibling, z)] + [(other, z) for other in others])
    sends = [
        transfer(own, out_ref.at[me], sems, k, (other, z)) for k, other in enumerate(others)
    ]
    pairs = [transfer(own, out_ref.at[me], pair_sems, 0, (sibling, z))]
    keep = pltpu.make_async_copy(own, out_ref.at[me], local_sems.at[2])
    keep.start()

    heads, width, tok = q_in.shape
    half = tok // 2
    loads[0].wait()

    def pack_heads(k, carry):
        a, b = q_in[2 * k], q_in[2 * k + 1]
        at = pl.ds(pl.multiple_of(k * tok, tok), tok)
        q_out[0, :, at] = jnp.concatenate([a[:, :half], b[:, :half]], axis=1)
        q_out[1, :, at] = jnp.concatenate([a[:, half:], b[:, half:]], axis=1)
        return carry

    lax.fori_loop(0, heads // 2, pack_heads, 0)
    loads[1].wait()
    for p in range(2):
        for lanes in range(g_wide.shape[0]):
            at = slice(lanes * LANES, (lanes + 1) * LANES)
            g_wide[lanes] = g_in[p * half * heads : (p + 1) * half * heads, at].astype(jnp.float32)
            for head in range(heads):
                g_out[p, head * half : (head + 1) * half, at] = g_wide[
                    lanes, pl.ds(head, half, stride=heads), :
                ].astype(g_out.dtype)

    for k in range(1, chips):
        sends[k - 1].wait_recv()
        owner = lax.rem(chip + chips - k, chips) * 2 + core
        pairs.append(
            transfer(out_ref.at[owner], out_ref.at[owner], pair_sems, k, (sibling, z))
        )
    for copy in sends:
        copy.wait_send()
    for copy in pairs:
        copy.wait()
    keep.wait()


def gather(latents, queries, grad_out, n_ctx):
    tok, width = latents.shape
    heads, lat = grad_out.shape[1:]
    total = heads * tok // 2
    vmem = pl.BlockSpec(memory_space=pltpu.VMEM)
    hbm = pl.BlockSpec(memory_space=pl.ANY)
    kind = latents.dtype
    out, q_cols, g_rows = pl.pallas_call(
        functools.partial(gather_kernel, n_ctx),
        in_specs=[vmem, hbm, hbm],
        out_specs=[hbm, vmem, vmem],
        out_shape=[
            jax.ShapeDtypeStruct((n_ctx, tok, width), kind),
            jax.ShapeDtypeStruct((2, width, total), kind),
            jax.ShapeDtypeStruct((2, total, lat), kind),
        ],
        scratch_shapes=[
            pltpu.VMEM((tok, width), kind),
            pltpu.VMEM((heads, width, tok), kind),
            pltpu.VMEM((tok * heads, lat), kind),
            pltpu.VMEM((lat // LANES, total, LANES), jnp.float32),
            pltpu.SemaphoreType.DMA((2, n_ctx // 2)),
            pltpu.SemaphoreType.DMA((2, n_ctx // 2)),
            pltpu.SemaphoreType.DMA((3,)),
        ],
        compiler_params=pltpu.CompilerParams(
            collective_id=0, has_side_effects=True, vmem_limit_bytes=32 * 1024 * 1024
        ),
    )(latents.T, jnp.transpose(queries, (1, 2, 0)), grad_out.reshape(tok * heads, lat))
    return out.reshape(n_ctx * tok, width), q_cols, g_rows


def reduce_kernel(
    n_ctx, n_head, part_ref, out_ref, pair_in, chip_out, chip_in, head_out, head_in, whole,
    pair_sems, chip_sems, head_sems, last_sems,
):
    me, core, chip, sibling, chips = places(n_ctx)
    z = lax.axis_index("head")
    others = [lax.rem(chip + k, chips) * 2 + core for k in range(1, chips)]
    heads = [lax.rem(z + k, n_head) for k in range(1, n_head)]
    greet(
        [(sibling, z)] + [(other, z) for other in others] + [(me, other) for other in heads]
    )
    order = [lax.rem(chip + k, chips) for k in range(1, chips + 1)]
    pairs = [
        transfer(
            part_ref.at[target * 2 + 1 - core], pair_in.at[k], pair_sems, k, (sibling, z)
        )
        for k, target in enumerate(order)
    ]
    sends = []
    total = None
    for k, target in enumerate(order):
        pairs[k].wait_recv()
        total = part_ref[target * 2 + core].astype(jnp.float32) + pair_in[k].astype(jnp.float32)
        if k < chips - 1:
            chip_out[k] = total.astype(jnp.bfloat16)
            sends.append(
                transfer(chip_out.at[k], chip_in.at[k], chip_sems, k, (others[k], z))
            )
    for k, copy in enumerate(sends):
        copy.wait_recv()
        total = total + chip_in[k].astype(jnp.float32)
    rows = total.shape[0] // n_head
    for k in range(n_head):
        head_out[k] = total[k * rows : (k + 1) * rows].astype(jnp.bfloat16)
    steps = [
        transfer(head_out.at[other], head_in.at[k], head_sems, k, (me, other))
        for k, other in enumerate(heads)
    ]
    piece = head_out[z].astype(jnp.float32)
    for k, copy in enumerate(steps):
        copy.wait_recv()
        piece = piece + head_in[k].astype(jnp.float32)
    whole[z] = piece.astype(jnp.bfloat16)
    lasts = [
        transfer(whole.at[z], whole.at[z], last_sems, k, (me, other))
        for k, other in enumerate(heads)
    ]
    for copy in lasts:
        copy.wait_recv()
    result = jnp.concatenate([whole[k] for k in range(n_head)], axis=0)
    out_ref[...] = result.astype(jnp.float32).T
    for copy in pairs + sends + steps + lasts:
        copy.wait_send()


def reduce_parts(parts, n_ctx, n_head):
    seq, width = parts.shape
    tok = seq // n_ctx
    rows = tok // n_head
    chips = n_ctx // 2
    kind = parts.dtype
    vmem = pl.BlockSpec(memory_space=pltpu.VMEM)
    out = pl.pallas_call(
        functools.partial(reduce_kernel, n_ctx, n_head),
        in_specs=[vmem],
        out_specs=vmem,
        out_shape=jax.ShapeDtypeStruct((width, tok), jnp.float32),
        scratch_shapes=[
            pltpu.VMEM((chips, tok, width), kind),
            pltpu.VMEM((chips, tok, width), kind),
            pltpu.VMEM((chips, tok, width), kind),
            pltpu.VMEM((n_head, rows, width), kind),
            pltpu.VMEM((n_head, rows, width), kind),
            pltpu.VMEM((n_head, rows, width), kind),
            pltpu.SemaphoreType.DMA((2, chips)),
            pltpu.SemaphoreType.DMA((2, chips)),
            pltpu.SemaphoreType.DMA((2, n_head)),
            pltpu.SemaphoreType.DMA((2, n_head)),
        ],
        compiler_params=pltpu.CompilerParams(
            collective_id=1, has_side_effects=True, vmem_limit_bytes=32 * 1024 * 1024
        ),
    )(parts.reshape(n_ctx, tok, width))
    return out.T


def body(queries, latents, grad_out, block_order, doc_ids):
    n_ctx = lax.axis_size("ctx")
    n_head = lax.axis_size("head")
    tok, heads, lat = grad_out.shape
    all_lat, q_cols, g_rows = gather(latents, queries, grad_out, n_ctx)
    out, gq, gl = attention(q_cols, g_rows, all_lat, block_order, doc_ids, n_ctx, heads)
    grad_latents = reduce_parts(gl, n_ctx, n_head)
    return out.reshape(tok, heads, lat), jnp.transpose(gq, (2, 0, 1)), grad_latents


def solution(mesh):
    return jax.shard_map(
        body,
        mesh=mesh,
        in_specs=(P("ctx", "head", None), P("ctx", None), P("ctx", "head", None), P(), P()),
        out_specs=(P("ctx", "head", None), P("ctx", "head", None), P("ctx", None)),
        check_vma=False,
    )
```

```python
import functools

import jax
import jax.numpy as jnp
from jax import lax
from jax.experimental import pallas as pl
from jax.experimental.pallas import tpu as pltpu
from jax.sharding import PartitionSpec as P

score_scale = 192.0 ** (-0.5)
far_below = -1e30
DOCS = 4
KEY_TILE = 256
COLS = 512
LANES = 128
NT = (((1,), (1,)), ((), ()))
NN = (((1,), (0,)), ((), ()))
TN = (((0,), (0,)), ((), ()))


def dot(a, b, dims):
    return lax.dot_general(a, b, dims, preferred_element_type=jnp.float32)


def attention_kernel(
    shape, order_ref, docs_ref, q_ref, g_ref, lat_ref, out_ref, gq_ref, gl_ref,
    keys, grad_keys, scores, grad_probs, out_acc, q_acc, by_token, bounds, sems,
):
    n_ctx, half, heads, cols, lat = shape
    seq = 2 * half * n_ctx
    part = pl.program_id(0)
    me = lax.axis_index("ctx")

    def block_of(slot):
        low = order_ref[slot // 2]
        return low if slot % 2 == 0 else 2 * n_ctx - 1 - low

    @pl.when(part == 0)
    def _():
        copies = []
        for slot in range(2 * n_ctx):
            first = pl.multiple_of(block_of(slot) * half, half)
            copy = pltpu.make_async_copy(
                lat_ref.at[pl.ds(slot * half, half)], keys.at[pl.ds(first, half)], sems.at[slot]
            )
            copy.start()
            copies.append(copy)
        keys[pl.ds(seq, KEY_TILE)] = jnp.zeros((KEY_TILE, keys.shape[1]), keys.dtype)
        grad_keys[...] = jnp.zeros_like(grad_keys)
        bounds[0] = 0
        for number in range(1, DOCS):
            at = jnp.int32(0)
            step = seq // 2
            while step >= 1:
                at = jnp.where(docs_ref[at + step - 1] < number, at + step, at)
                step //= 2
            bounds[number] = at
        for copy in copies:
            copy.wait()

    low = order_ref[me]
    pos0 = jnp.where(part == 0, low, 2 * n_ctx - 1 - low) * half
    doc_start = jnp.int32(0)
    for number in range(1, DOCS):
        doc_start = jnp.where(bounds[number] <= pos0, bounds[number], doc_start)
    start = (doc_start // 16) * 16
    tiles = (pos0 + half - start + KEY_TILE - 1) // KEY_TILE

    row_pos = pos0 + lax.rem(lax.broadcasted_iota(jnp.int32, (1, cols), 1), half)
    row_doc = jnp.zeros_like(row_pos)
    for number in range(1, DOCS):
        row_doc = jnp.where(bounds[number] <= row_pos, bounds[number], row_doc)

    def tile_at(i):
        return pl.ds(pl.multiple_of(start + i * KEY_TILE, 16), KEY_TILE)

    heads_now = cols // half
    for chunk in range(heads * half // cols):
        here = slice(chunk * cols, (chunk + 1) * cols)

        def first_pass(i, row_max):
            at = tile_at(i)
            s = dot(keys[at, :], q_ref[0, :, here], NN) * score_scale
            key_pos = start + i * KEY_TILE + lax.broadcasted_iota(jnp.int32, (KEY_TILE, 1), 0)
            s = jnp.where((key_pos <= row_pos) & (key_pos >= row_doc), s, far_below)
            scores[i] = s
            grad_probs[i] = dot(keys[at, :lat], g_ref[0, here, :], NT)
            return jnp.maximum(row_max, jnp.max(s, axis=0, keepdims=True))

        row_max = lax.fori_loop(
            0, tiles, first_pass, jnp.full((1, cols), far_below, jnp.float32)
        )

        def second_pass(i, sums):
            row_sum, weighted = sums
            e = jnp.exp(scores[i] - row_max)
            scores[i] = e
            return (
                row_sum + jnp.sum(e, axis=0, keepdims=True),
                weighted + jnp.sum(e * grad_probs[i], axis=0, keepdims=True),
            )

        zero = jnp.zeros((1, cols), jnp.float32)
        row_sum, weighted = lax.fori_loop(0, tiles, second_pass, (zero, zero))
        inverse = 1.0 / row_sum
        delta = weighted * inverse
        scaled = inverse * score_scale
        out_acc[...] = jnp.zeros_like(out_acc)
        q_acc[...] = jnp.zeros_like(q_acc)

        def third_pass(i, carry):
            at = tile_at(i)
            e = scores[i]
            probs = (e * inverse).astype(jnp.bfloat16)
            ds = (e * scaled * (grad_probs[i] - delta)).astype(jnp.bfloat16)
            out_acc[...] += dot(probs, keys[at, :lat], TN)
            q_acc[...] += dot(keys[at, :], ds, TN)
            key_term = dot(ds, q_ref[0, :, here], NT)
            value_term = dot(probs, g_ref[0, here, :], NN)
            grad_keys[at, :lat] += key_term[:, :lat] + value_term
            grad_keys[at, lat:] += key_term[:, lat:]
            return carry

        lax.fori_loop(0, tiles, third_pass, 0)
        for k in range(heads_now):
            head = chunk * heads_now + k
            mine = slice(k * half, (k + 1) * half)
            for lanes in range(lat // LANES):
                by_token[lanes, pl.ds(head, half, stride=heads), :] = out_acc[
                    mine, lanes * LANES : (lanes + 1) * LANES
                ]

        for p in range(2):
            @pl.when(part == p)
            def _():
                for k in range(heads_now):
                    head = chunk * heads_now + k
                    mine = slice(k * half, (k + 1) * half)
                    gq_ref[head, :, p * half : (p + 1) * half] = q_acc[:, mine].astype(
                        gq_ref.dtype
                    )

    for lanes in range(lat // LANES):
        out_ref[:, lanes * LANES : (lanes + 1) * LANES] = by_token[lanes].astype(out_ref.dtype)

    @pl.when(part == 1)
    def _():
        for slot in range(2 * n_ctx):
            first = pl.multiple_of(block_of(slot) * half, half)
            gl_ref[pl.ds(slot * half, half), :] = grad_keys[pl.ds(first, half), :].astype(
                gl_ref.dtype
            )


def attention(q_cols, g_rows, all_lat, block_order, doc_ids, n_ctx, heads):
    width, total = q_cols.shape[1:]
    lat = g_rows.shape[2]
    half = total // heads
    tok = 2 * half
    seq = tok * n_ctx
    cols = min(total, COLS)
    tile_count = seq // KEY_TILE + 1
    return pl.pallas_call(
        functools.partial(attention_kernel, (n_ctx, half, heads, cols, lat)),
        grid_spec=pltpu.PrefetchScalarGridSpec(
            num_scalar_prefetch=2,
            grid=(2,),
            in_specs=[
                pl.BlockSpec((1, width, total), lambda p, *_: (p, 0, 0)),
                pl.BlockSpec((1, total, lat), lambda p, *_: (p, 0, 0)),
                pl.BlockSpec(memory_space=pl.ANY),
            ],
            out_specs=[
                pl.BlockSpec((total, lat), lambda p, *_: (p, 0)),
                pl.BlockSpec((heads, width, tok), lambda p, *_: (0, 0, 0)),
                pl.BlockSpec((seq, width), lambda p, *_: (0, 0)),
            ],
            scratch_shapes=[
                pltpu.VMEM((seq + KEY_TILE, width), jnp.bfloat16),
                pltpu.VMEM((seq + KEY_TILE, width), jnp.float32),
                pltpu.VMEM((tile_count, KEY_TILE, cols), jnp.float32),
                pltpu.VMEM((tile_count, KEY_TILE, cols), jnp.float32),
                pltpu.VMEM((cols, lat), jnp.float32),
                pltpu.VMEM((width, cols), jnp.float32),
                pltpu.VMEM((lat // LANES, total, LANES), jnp.float32),
                pltpu.SMEM((DOCS,), jnp.int32),
                pltpu.SemaphoreType.DMA((2 * n_ctx,)),
            ],
        ),
        out_shape=[
            jax.ShapeDtypeStruct((tok * heads, lat), jnp.bfloat16),
            jax.ShapeDtypeStruct((heads, width, tok), jnp.bfloat16),
            jax.ShapeDtypeStruct((seq, width), jnp.bfloat16),
        ],
        compiler_params=pltpu.CompilerParams(vmem_limit_bytes=56 * 1024 * 1024),
        cost_estimate=pl.CostEstimate(
            flops=14 * tok * heads * seq * lat // 2, bytes_accessed=12 << 20, transcendentals=0
        ),
    )(block_order, doc_ids, q_cols, g_rows, all_lat)


def transfer(src, dst, sems, index, device):
    copy = pltpu.make_async_remote_copy(
        src_ref=src, dst_ref=dst, send_sem=sems.at[0, index], recv_sem=sems.at[1, index],
        device_id=device, device_id_type=pl.DeviceIdType.MESH,
    )
    copy.start()
    return copy


def greet(peers):
    barrier = pltpu.get_barrier_semaphore()
    for peer in peers:
        pl.semaphore_signal(
            barrier, inc=1, device_id=peer, device_id_type=pl.DeviceIdType.MESH
        )
    pl.semaphore_wait(barrier, len(peers))


def places(n_ctx):
    me = lax.axis_index("ctx")
    core = lax.rem(me, 2)
    chip = me // 2
    sibling = chip * 2 + 1 - core
    chips = n_ctx // 2
    return me, core, chip, sibling, chips


def gather_kernel(
    n_ctx, lat_ref, q_hbm, g_hbm, out_ref, q_hbm_out, g_hbm_out, own, q_in, g_in, q_out,
    g_out, g_wide,
    sems, pair_sems, local_sems,
):
    me, core, chip, sibling, chips = places(n_ctx)
    z = lax.axis_index("head")
    others = [lax.rem(chip + k, chips) * 2 + core for k in range(1, chips)]
    loads = [
        pltpu.make_async_copy(q_hbm, q_in, local_sems.at[0]),
        pltpu.make_async_copy(g_hbm, g_in, local_sems.at[1]),
    ]
    for load in loads:
        load.start()
    own[...] = lat_ref[...].T
    greet([(sibling, z)] + [(other, z) for other in others])
    sends = [
        transfer(own, out_ref.at[me], sems, k, (other, z)) for k, other in enumerate(others)
    ]
    pairs = [transfer(own, out_ref.at[me], pair_sems, 0, (sibling, z))]
    keep = pltpu.make_async_copy(own, out_ref.at[me], local_sems.at[2])
    keep.start()

    heads, width, tok = q_in.shape
    half = tok // 2
    loads[0].wait()

    def pack_heads(k, carry):
        a, b = q_in[2 * k], q_in[2 * k + 1]
        at = pl.ds(pl.multiple_of(k * tok, tok), tok)
        q_out[0, :, at] = jnp.concatenate([a[:, :half], b[:, :half]], axis=1)
        q_out[1, :, at] = jnp.concatenate([a[:, half:], b[:, half:]], axis=1)
        return carry

    lax.fori_loop(0, heads // 2, pack_heads, 0)
    stores = [
        pltpu.make_async_copy(q_out, q_hbm_out, local_sems.at[3]),
        pltpu.make_async_copy(g_out, g_hbm_out, local_sems.at[4]),
    ]
    stores[0].start()
    loads[1].wait()
    for p in range(2):
        for lanes in range(g_wide.shape[0]):
            at = slice(lanes * LANES, (lanes + 1) * LANES)
            g_wide[lanes] = g_in[p * half * heads : (p + 1) * half * heads, at].astype(jnp.float32)
            for head in range(heads):
                g_out[p, head * half : (head + 1) * half, at] = g_wide[
                    lanes, pl.ds(head, half, stride=heads), :
                ].astype(g_out.dtype)

    stores[1].start()
    for k in range(1, chips):
        sends[k - 1].wait_recv()
        owner = lax.rem(chip + chips - k, chips) * 2 + core
        pairs.append(
            transfer(out_ref.at[owner], out_ref.at[owner], pair_sems, k, (sibling, z))
        )
    for copy in sends:
        copy.wait_send()
    for copy in pairs:
        copy.wait()
    for copy in stores:
        copy.wait()
    keep.wait()


def gather(latents, queries, grad_out, n_ctx):
    tok, width = latents.shape
    heads, lat = grad_out.shape[1:]
    total = heads * tok // 2
    vmem = pl.BlockSpec(memory_space=pltpu.VMEM)
    hbm = pl.BlockSpec(memory_space=pl.ANY)
    kind = latents.dtype
    out, q_cols, g_rows = pl.pallas_call(
        functools.partial(gather_kernel, n_ctx),
        in_specs=[vmem, hbm, hbm],
        out_specs=[hbm, hbm, hbm],
        out_shape=[
            jax.ShapeDtypeStruct((n_ctx, tok, width), kind),
            jax.ShapeDtypeStruct((2, width, total), kind),
            jax.ShapeDtypeStruct((2, total, lat), kind),
        ],
        scratch_shapes=[
            pltpu.VMEM((tok, width), kind),
            pltpu.VMEM((heads, width, tok), kind),
            pltpu.VMEM((tok * heads, lat), kind),
            pltpu.VMEM((2, width, total), kind),
            pltpu.VMEM((2, total, lat), kind),
            pltpu.VMEM((lat // LANES, total, LANES), jnp.float32),
            pltpu.SemaphoreType.DMA((2, n_ctx // 2)),
            pltpu.SemaphoreType.DMA((2, n_ctx // 2)),
            pltpu.SemaphoreType.DMA((5,)),
        ],
        compiler_params=pltpu.CompilerParams(
            collective_id=0, has_side_effects=True, vmem_limit_bytes=56 * 1024 * 1024
        ),
    )(latents.T, jnp.transpose(queries, (1, 2, 0)), grad_out.reshape(tok * heads, lat))
    return out.reshape(n_ctx * tok, width), q_cols, g_rows


def reduce_kernel(
    n_ctx, n_head, part_ref, out_ref, pair_in, chip_out, chip_in, head_out, head_in, whole, sum_own,
    pair_sems, chip_sems, head_sems, last_sems,
):
    me, core, chip, sibling, chips = places(n_ctx)
    z = lax.axis_index("head")
    others = [lax.rem(chip + k, chips) * 2 + core for k in range(1, chips)]
    heads = [lax.rem(z + k, n_head) for k in range(1, n_head)]
    greet(
        [(sibling, z)] + [(other, z) for other in others] + [(me, other) for other in heads]
    )
    order = [lax.rem(chip + k, chips) for k in range(1, chips + 1)]
    parts = part_ref.shape[1]
    rows = part_ref.shape[2] // n_head
    pairs = [
        [
            transfer(
                part_ref.at[target * 2 + 1 - core, s], pair_in.at[s, k], pair_sems.at[s], k,
                (sibling, z),
            )
            for k, target in enumerate(order)
        ]
        for s in range(parts)
    ]
    sends, steps, lasts, totals = [], [], [], []
    for s in range(parts):
        sent = []
        for k, target in enumerate(order):
            pairs[s][k].wait_recv()
            total = part_ref[target * 2 + core, s].astype(jnp.float32) + pair_in[s, k].astype(
                jnp.float32
            )
            if k < chips - 1:
                chip_out[s, k] = total.astype(jnp.bfloat16)
                sent.append(
                    transfer(
                        chip_out.at[s, k], chip_in.at[s, k], chip_sems.at[s], k, (others[k], z)
                    )
                )
        sum_own[s] = total
        sends.append(sent)
    for s in range(parts):
        total = sum_own[s]
        for k, copy in enumerate(sends[s]):
            copy.wait_recv()
            total = total + chip_in[s, k].astype(jnp.float32)
        for k in range(n_head):
            head_out[s, k] = total[k * rows : (k + 1) * rows].astype(jnp.bfloat16)
        steps.append([
            transfer(head_out.at[s, other], head_in.at[s, k], head_sems.at[s], k, (me, other))
            for k, other in enumerate(heads)
        ])
    for s in range(parts):
        piece = head_out[s, z].astype(jnp.float32)
        for k, copy in enumerate(steps[s]):
            copy.wait_recv()
            piece = piece + head_in[s, k].astype(jnp.float32)
        whole[s, z] = piece.astype(jnp.bfloat16)
        lasts.append([
            transfer(whole.at[s, z], whole.at[s, z], last_sems.at[s], k, (me, other))
            for k, other in enumerate(heads)
        ])
    for copies in lasts:
        for copy in copies:
            copy.wait_recv()
    result = jnp.concatenate(
        [whole[s, k] for s in range(parts) for k in range(n_head)], axis=0
    )
    out_ref[...] = result.astype(jnp.float32).T
    for copies in pairs + sends + steps + lasts:
        for copy in copies:
            copy.wait_send()


def reduce_parts(parts, n_ctx, n_head):
    seq, width = parts.shape
    tok = seq // n_ctx
    splits = 2 if tok // (2 * n_head) >= 16 else 1
    deep = tok // splits
    rows = deep // n_head
    chips = n_ctx // 2
    kind = parts.dtype
    vmem = pl.BlockSpec(memory_space=pltpu.VMEM)
    out = pl.pallas_call(
        functools.partial(reduce_kernel, n_ctx, n_head),
        in_specs=[vmem],
        out_specs=vmem,
        out_shape=jax.ShapeDtypeStruct((width, tok), jnp.float32),
        scratch_shapes=[
            pltpu.VMEM((splits, chips, deep, width), kind),
            pltpu.VMEM((splits, chips, deep, width), kind),
            pltpu.VMEM((splits, chips, deep, width), kind),
            pltpu.VMEM((splits, n_head, rows, width), kind),
            pltpu.VMEM((splits, n_head, rows, width), kind),
            pltpu.VMEM((splits, n_head, rows, width), kind),
            pltpu.VMEM((splits, deep, width), jnp.float32),
            pltpu.SemaphoreType.DMA((splits, 2, chips)),
            pltpu.SemaphoreType.DMA((splits, 2, chips)),
            pltpu.SemaphoreType.DMA((splits, 2, n_head)),
            pltpu.SemaphoreType.DMA((splits, 2, n_head)),
        ],
        compiler_params=pltpu.CompilerParams(
            collective_id=1, has_side_effects=True, vmem_limit_bytes=32 * 1024 * 1024
        ),
    )(parts.reshape(n_ctx, splits, deep, width))
    return out.T


def body(queries, latents, grad_out, block_order, doc_ids):
    n_ctx = lax.axis_size("ctx")
    n_head = lax.axis_size("head")
    tok, heads, lat = grad_out.shape
    all_lat, q_cols, g_rows = gather(latents, queries, grad_out, n_ctx)
    out, gq, gl = attention(q_cols, g_rows, all_lat, block_order, doc_ids, n_ctx, heads)
    grad_latents = reduce_parts(gl, n_ctx, n_head)
    return out.reshape(tok, heads, lat), jnp.transpose(gq, (2, 0, 1)), grad_latents


def solution(mesh):
    return jax.shard_map(
        body,
        mesh=mesh,
        in_specs=(P("ctx", "head", None), P("ctx", None), P("ctx", "head", None), P(), P()),
        out_specs=(P("ctx", "head", None), P("ctx", "head", None), P("ctx", None)),
        check_vma=False,
    )
```

```python
import functools

import jax
import jax.numpy as jnp
from jax import lax
from jax.experimental import pallas as pl
from jax.experimental.pallas import tpu as pltpu
from jax.sharding import PartitionSpec as P

score_scale = 192.0 ** (-0.5)
far_below = -1e30
DOCS = 4
KEY_TILE = 256
COLS = 1024
LANES = 128
NT = (((1,), (1,)), ((), ()))
NN = (((1,), (0,)), ((), ()))
TN = (((0,), (0,)), ((), ()))


def dot(a, b, dims):
    return lax.dot_general(a, b, dims, preferred_element_type=jnp.float32)


def attention_kernel(
    shape, order_ref, docs_ref, q_ref, g_ref, lat_ref, out_ref, gq_ref, gl_ref,
    keys, grad_keys, scores, grad_probs, out_acc, q_acc, by_token, bounds, sems,
):
    n_ctx, half, heads, cols, lat = shape
    seq = 2 * half * n_ctx
    part = pl.program_id(0)
    me = lax.axis_index("ctx")

    def block_of(slot):
        low = order_ref[slot // 2]
        return low if slot % 2 == 0 else 2 * n_ctx - 1 - low

    @pl.when(part == 0)
    def _():
        copies = []
        for slot in range(2 * n_ctx):
            first = pl.multiple_of(block_of(slot) * half, half)
            copy = pltpu.make_async_copy(
                lat_ref.at[pl.ds(slot * half, half)], keys.at[pl.ds(first, half)], sems.at[slot]
            )
            copy.start()
            copies.append(copy)
        keys[pl.ds(seq, KEY_TILE)] = jnp.zeros((KEY_TILE, keys.shape[1]), keys.dtype)
        grad_keys[...] = jnp.zeros_like(grad_keys)
        bounds[0] = 0
        for number in range(1, DOCS):
            at = jnp.int32(0)
            step = seq // 2
            while step >= 1:
                at = jnp.where(docs_ref[at + step - 1] < number, at + step, at)
                step //= 2
            bounds[number] = at
        for copy in copies:
            copy.wait()

    low = order_ref[me]
    pos0 = jnp.where(part == 0, low, 2 * n_ctx - 1 - low) * half
    doc_start = jnp.int32(0)
    for number in range(1, DOCS):
        doc_start = jnp.where(bounds[number] <= pos0, bounds[number], doc_start)
    start = (doc_start // 16) * 16
    tiles = (pos0 + half - start + KEY_TILE - 1) // KEY_TILE

    row_pos = pos0 + lax.rem(lax.broadcasted_iota(jnp.int32, (1, cols), 1), half)
    row_doc = jnp.zeros_like(row_pos)
    for number in range(1, DOCS):
        row_doc = jnp.where(bounds[number] <= row_pos, bounds[number], row_doc)

    def tile_at(i):
        return pl.ds(pl.multiple_of(start + i * KEY_TILE, 16), KEY_TILE)

    heads_now = cols // half
    for chunk in range(heads * half // cols):
        here = slice(chunk * cols, (chunk + 1) * cols)

        def first_pass(i, row_max):
            at = tile_at(i)
            s = dot(keys[at, :], q_ref[0, :, here], NN) * score_scale
            key_pos = start + i * KEY_TILE + lax.broadcasted_iota(jnp.int32, (KEY_TILE, 1), 0)
            s = jnp.where((key_pos <= row_pos) & (key_pos >= row_doc), s, far_below)
            scores[i] = s
            grad_probs[i] = dot(keys[at, :lat], g_ref[0, here, :], NT)
            return jnp.maximum(row_max, jnp.max(s, axis=0, keepdims=True))

        row_max = lax.fori_loop(
            0, tiles, first_pass, jnp.full((1, cols), far_below, jnp.float32)
        )

        def second_pass(i, sums):
            row_sum, weighted = sums
            e = jnp.exp(scores[i] - row_max)
            scores[i] = e
            return (
                row_sum + jnp.sum(e, axis=0, keepdims=True),
                weighted + jnp.sum(e * grad_probs[i], axis=0, keepdims=True),
            )

        zero = jnp.zeros((1, cols), jnp.float32)
        row_sum, weighted = lax.fori_loop(0, tiles, second_pass, (zero, zero))
        inverse = 1.0 / row_sum
        delta = weighted * inverse
        scaled = inverse * score_scale

        def third_pass(i, first):
            at = tile_at(i)
            e = scores[i]
            probs = (e * inverse).astype(jnp.bfloat16)
            ds = (e * scaled * (grad_probs[i] - delta)).astype(jnp.bfloat16)
            out_now = dot(probs, keys[at, :lat], TN)
            q_now = dot(keys[at, :], ds, TN)
            out_acc[...] = out_now if first else out_acc[...] + out_now
            q_acc[...] = q_now if first else q_acc[...] + q_now
            key_term = dot(ds, q_ref[0, :, here], NT)
            value_term = dot(probs, g_ref[0, here, :], NN)
            grad_keys[at, :lat] += key_term[:, :lat] + value_term
            grad_keys[at, lat:] += key_term[:, lat:]

        third_pass(0, True)

        @pl.loop(1, tiles)
        def _(i):
            third_pass(i, False)

        for k in range(heads_now):
            head = chunk * heads_now + k
            mine = slice(k * half, (k + 1) * half)
            for lanes in range(lat // LANES):
                by_token[lanes, pl.ds(head, half, stride=heads), :] = out_acc[
                    mine, lanes * LANES : (lanes + 1) * LANES
                ]

        for p in range(2):
            @pl.when(part == p)
            def _():
                for k in range(heads_now):
                    head = chunk * heads_now + k
                    mine = slice(k * half, (k + 1) * half)
                    gq_ref[head, :, p * half : (p + 1) * half] = q_acc[:, mine].astype(
                        gq_ref.dtype
                    )

    for lanes in range(lat // LANES):
        out_ref[:, lanes * LANES : (lanes + 1) * LANES] = by_token[lanes].astype(out_ref.dtype)

    @pl.when(part == 1)
    def _():
        for slot in range(2 * n_ctx):
            first = pl.multiple_of(block_of(slot) * half, half)
            gl_ref[pl.ds(slot * half, half), :] = grad_keys[pl.ds(first, half), :].astype(
                gl_ref.dtype
            )


def attention(q_cols, g_rows, all_lat, block_order, doc_ids, n_ctx, heads):
    width, total = q_cols.shape[1:]
    lat = g_rows.shape[2]
    half = total // heads
    tok = 2 * half
    seq = tok * n_ctx
    cols = min(total, COLS)
    tile_count = seq // KEY_TILE + 1
    return pl.pallas_call(
        functools.partial(attention_kernel, (n_ctx, half, heads, cols, lat)),
        grid_spec=pltpu.PrefetchScalarGridSpec(
            num_scalar_prefetch=2,
            grid=(2,),
            in_specs=[
                pl.BlockSpec((1, width, total), lambda p, *_: (p, 0, 0)),
                pl.BlockSpec((1, total, lat), lambda p, *_: (p, 0, 0)),
                pl.BlockSpec(memory_space=pl.ANY),
            ],
            out_specs=[
                pl.BlockSpec((total, lat), lambda p, *_: (p, 0)),
                pl.BlockSpec((heads, width, tok), lambda p, *_: (0, 0, 0)),
                pl.BlockSpec((seq, width), lambda p, *_: (0, 0)),
            ],
            scratch_shapes=[
                pltpu.VMEM((seq + KEY_TILE, width), jnp.bfloat16),
                pltpu.VMEM((seq + KEY_TILE, width), jnp.float32),
                pltpu.VMEM((tile_count, KEY_TILE, cols), jnp.float32),
                pltpu.VMEM((tile_count, KEY_TILE, cols), jnp.float32),
                pltpu.VMEM((cols, lat), jnp.float32),
                pltpu.VMEM((width, cols), jnp.float32),
                pltpu.VMEM((lat // LANES, total, LANES), jnp.float32),
                pltpu.SMEM((DOCS,), jnp.int32),
                pltpu.SemaphoreType.DMA((2 * n_ctx,)),
            ],
        ),
        out_shape=[
            jax.ShapeDtypeStruct((tok * heads, lat), jnp.bfloat16),
            jax.ShapeDtypeStruct((heads, width, tok), jnp.bfloat16),
            jax.ShapeDtypeStruct((seq, width), jnp.bfloat16),
        ],
        compiler_params=pltpu.CompilerParams(vmem_limit_bytes=56 * 1024 * 1024),
        cost_estimate=pl.CostEstimate(
            flops=14 * tok * heads * seq * lat // 2, bytes_accessed=12 << 20, transcendentals=0
        ),
    )(block_order, doc_ids, q_cols, g_rows, all_lat)


def transfer(src, dst, sems, index, device):
    copy = pltpu.make_async_remote_copy(
        src_ref=src, dst_ref=dst, send_sem=sems.at[0, index], recv_sem=sems.at[1, index],
        device_id=device, device_id_type=pl.DeviceIdType.MESH,
    )
    copy.start()
    return copy


def greet(peers):
    barrier = pltpu.get_barrier_semaphore()
    for peer in peers:
        pl.semaphore_signal(
            barrier, inc=1, device_id=peer, device_id_type=pl.DeviceIdType.MESH
        )
    pl.semaphore_wait(barrier, len(peers))


def places(n_ctx):
    me = lax.axis_index("ctx")
    core = lax.rem(me, 2)
    chip = me // 2
    sibling = chip * 2 + 1 - core
    chips = n_ctx // 2
    return me, core, chip, sibling, chips


def gather_kernel(
    n_ctx, lat_ref, q_hbm, g_hbm, out_ref, q_hbm_out, g_hbm_out, own, q_in, g_in, q_out,
    g_out, g_wide,
    sems, pair_sems, local_sems,
):
    me, core, chip, sibling, chips = places(n_ctx)
    z = lax.axis_index("head")
    others = [lax.rem(chip + k, chips) * 2 + core for k in range(1, chips)]
    loads = [
        pltpu.make_async_copy(q_hbm, q_in, local_sems.at[0]),
        pltpu.make_async_copy(g_hbm, g_in, local_sems.at[1]),
    ]
    for load in loads:
        load.start()
    own[...] = lat_ref[...].T
    greet([(sibling, z)] + [(other, z) for other in others])
    sends = [
        transfer(own, out_ref.at[me], sems, k, (other, z)) for k, other in enumerate(others)
    ]
    pairs = [transfer(own, out_ref.at[me], pair_sems, 0, (sibling, z))]
    keep = pltpu.make_async_copy(own, out_ref.at[me], local_sems.at[2])
    keep.start()

    heads, width, tok = q_in.shape
    half = tok // 2
    loads[0].wait()

    def pack_heads(k, carry):
        a, b = q_in[2 * k], q_in[2 * k + 1]
        at = pl.ds(pl.multiple_of(k * tok, tok), tok)
        q_out[0, :, at] = jnp.concatenate([a[:, :half], b[:, :half]], axis=1)
        q_out[1, :, at] = jnp.concatenate([a[:, half:], b[:, half:]], axis=1)
        return carry

    lax.fori_loop(0, heads // 2, pack_heads, 0)
    stores = [
        pltpu.make_async_copy(q_out, q_hbm_out, local_sems.at[3]),
        pltpu.make_async_copy(g_out, g_hbm_out, local_sems.at[4]),
    ]
    stores[0].start()
    loads[1].wait()
    for p in range(2):
        for lanes in range(g_wide.shape[0]):
            at = slice(lanes * LANES, (lanes + 1) * LANES)
            g_wide[lanes] = g_in[p * half * heads : (p + 1) * half * heads, at].astype(jnp.float32)
            for head in range(heads):
                g_out[p, head * half : (head + 1) * half, at] = g_wide[
                    lanes, pl.ds(head, half, stride=heads), :
                ].astype(g_out.dtype)

    stores[1].start()
    for k in range(1, chips):
        sends[k - 1].wait_recv()
        owner = lax.rem(chip + chips - k, chips) * 2 + core
        pairs.append(
            transfer(out_ref.at[owner], out_ref.at[owner], pair_sems, k, (sibling, z))
        )
    for copy in sends:
        copy.wait_send()
    for copy in pairs:
        copy.wait()
    for copy in stores:
        copy.wait()
    keep.wait()


def gather(latents, queries, grad_out, n_ctx):
    tok, width = latents.shape
    heads, lat = grad_out.shape[1:]
    total = heads * tok // 2
    vmem = pl.BlockSpec(memory_space=pltpu.VMEM)
    hbm = pl.BlockSpec(memory_space=pl.ANY)
    kind = latents.dtype
    out, q_cols, g_rows = pl.pallas_call(
        functools.partial(gather_kernel, n_ctx),
        in_specs=[vmem, hbm, hbm],
        out_specs=[hbm, hbm, hbm],
        out_shape=[
            jax.ShapeDtypeStruct((n_ctx, tok, width), kind),
            jax.ShapeDtypeStruct((2, width, total), kind),
            jax.ShapeDtypeStruct((2, total, lat), kind),
        ],
        scratch_shapes=[
            pltpu.VMEM((tok, width), kind),
            pltpu.VMEM((heads, width, tok), kind),
            pltpu.VMEM((tok * heads, lat), kind),
            pltpu.VMEM((2, width, total), kind),
            pltpu.VMEM((2, total, lat), kind),
            pltpu.VMEM((lat // LANES, total, LANES), jnp.float32),
            pltpu.SemaphoreType.DMA((2, n_ctx // 2)),
            pltpu.SemaphoreType.DMA((2, n_ctx // 2)),
            pltpu.SemaphoreType.DMA((5,)),
        ],
        compiler_params=pltpu.CompilerParams(
            collective_id=0, has_side_effects=True, vmem_limit_bytes=56 * 1024 * 1024
        ),
    )(latents.T, jnp.transpose(queries, (1, 2, 0)), grad_out.reshape(tok * heads, lat))
    return out.reshape(n_ctx * tok, width), q_cols, g_rows


def reduce_kernel(
    n_ctx, n_head, part_ref, out_ref, pair_in, chip_out, chip_in, head_out, head_in, whole, sum_own,
    pair_sems, chip_sems, head_sems, last_sems,
):
    me, core, chip, sibling, chips = places(n_ctx)
    z = lax.axis_index("head")
    others = [lax.rem(chip + k, chips) * 2 + core for k in range(1, chips)]
    heads = [lax.rem(z + k, n_head) for k in range(1, n_head)]
    greet(
        [(sibling, z)] + [(other, z) for other in others] + [(me, other) for other in heads]
    )
    order = [lax.rem(chip + k, chips) for k in range(1, chips + 1)]
    parts = part_ref.shape[1]
    rows = part_ref.shape[2] // n_head
    pairs = [
        [
            transfer(
                part_ref.at[target * 2 + 1 - core, s], pair_in.at[s, k], pair_sems.at[s], k,
                (sibling, z),
            )
            for k, target in enumerate(order)
        ]
        for s in range(parts)
    ]
    sends, steps, lasts, totals = [], [], [], []
    for s in range(parts):
        sent = []
        for k, target in enumerate(order):
            pairs[s][k].wait_recv()
            total = part_ref[target * 2 + core, s].astype(jnp.float32) + pair_in[s, k].astype(
                jnp.float32
            )
            if k < chips - 1:
                chip_out[s, k] = total.astype(jnp.bfloat16)
                sent.append(
                    transfer(
                        chip_out.at[s, k], chip_in.at[s, k], chip_sems.at[s], k, (others[k], z)
                    )
                )
        sum_own[s] = total
        sends.append(sent)
    for s in range(parts):
        total = sum_own[s]
        for k, copy in enumerate(sends[s]):
            copy.wait_recv()
            total = total + chip_in[s, k].astype(jnp.float32)
        for k in range(n_head):
            head_out[s, k] = total[k * rows : (k + 1) * rows].astype(jnp.bfloat16)
        steps.append([
            transfer(head_out.at[s, other], head_in.at[s, k], head_sems.at[s], k, (me, other))
            for k, other in enumerate(heads)
        ])
    for s in range(parts):
        piece = head_out[s, z].astype(jnp.float32)
        for k, copy in enumerate(steps[s]):
            copy.wait_recv()
            piece = piece + head_in[s, k].astype(jnp.float32)
        whole[s, z] = piece.astype(jnp.bfloat16)
        lasts.append([
            transfer(whole.at[s, z], whole.at[s, z], last_sems.at[s], k, (me, other))
            for k, other in enumerate(heads)
        ])
    for copies in lasts:
        for copy in copies:
            copy.wait_recv()
    result = jnp.concatenate(
        [whole[s, k] for s in range(parts) for k in range(n_head)], axis=0
    )
    out_ref[...] = result.astype(jnp.float32).T
    for copies in pairs + sends + steps + lasts:
        for copy in copies:
            copy.wait_send()


def reduce_parts(parts, n_ctx, n_head):
    seq, width = parts.shape
    tok = seq // n_ctx
    splits = 2 if tok // (2 * n_head) >= 16 else 1
    deep = tok // splits
    rows = deep // n_head
    chips = n_ctx // 2
    kind = parts.dtype
    vmem = pl.BlockSpec(memory_space=pltpu.VMEM)
    out = pl.pallas_call(
        functools.partial(reduce_kernel, n_ctx, n_head),
        in_specs=[vmem],
        out_specs=vmem,
        out_shape=jax.ShapeDtypeStruct((width, tok), jnp.float32),
        scratch_shapes=[
            pltpu.VMEM((splits, chips, deep, width), kind),
            pltpu.VMEM((splits, chips, deep, width), kind),
            pltpu.VMEM((splits, chips, deep, width), kind),
            pltpu.VMEM((splits, n_head, rows, width), kind),
            pltpu.VMEM((splits, n_head, rows, width), kind),
            pltpu.VMEM((splits, n_head, rows, width), kind),
            pltpu.VMEM((splits, deep, width), jnp.float32),
            pltpu.SemaphoreType.DMA((splits, 2, chips)),
            pltpu.SemaphoreType.DMA((splits, 2, chips)),
            pltpu.SemaphoreType.DMA((splits, 2, n_head)),
            pltpu.SemaphoreType.DMA((splits, 2, n_head)),
        ],
        compiler_params=pltpu.CompilerParams(
            collective_id=1, has_side_effects=True, vmem_limit_bytes=32 * 1024 * 1024
        ),
    )(parts.reshape(n_ctx, splits, deep, width))
    return out.T


def body(queries, latents, grad_out, block_order, doc_ids):
    n_ctx = lax.axis_size("ctx")
    n_head = lax.axis_size("head")
    tok, heads, lat = grad_out.shape
    all_lat, q_cols, g_rows = gather(latents, queries, grad_out, n_ctx)
    out, gq, gl = attention(q_cols, g_rows, all_lat, block_order, doc_ids, n_ctx, heads)
    grad_latents = reduce_parts(gl, n_ctx, n_head)
    return out.reshape(tok, heads, lat), jnp.transpose(gq, (2, 0, 1)), grad_latents


def solution(mesh):
    return jax.shard_map(
        body,
        mesh=mesh,
        in_specs=(P("ctx", "head", None), P("ctx", None), P("ctx", "head", None), P(), P()),
        out_specs=(P("ctx", "head", None), P("ctx", "head", None), P("ctx", None)),
        check_vma=False,
    )
```

```python
import functools

import jax
import jax.numpy as jnp
from jax import lax
from jax.experimental import pallas as pl
from jax.experimental.pallas import tpu as pltpu
from jax.sharding import PartitionSpec as P

score_scale = 192.0 ** (-0.5)
far_below = -1e30
DOCS = 4
KEY_TILE = 256
COLS = 1024
LANES = 128
NT = (((1,), (1,)), ((), ()))
NN = (((1,), (0,)), ((), ()))
TN = (((0,), (0,)), ((), ()))


def dot(a, b, dims):
    return lax.dot_general(a, b, dims, preferred_element_type=jnp.float32)


def attention_kernel(
    shape, order_ref, docs_ref, q_ref, g_ref, lat_ref, out_ref, gq_ref, gl_ref,
    keys, grad_keys, scores, grad_probs, out_acc, q_acc, by_token, bounds, sems,
):
    n_ctx, half, heads, cols, lat = shape
    seq = 2 * half * n_ctx
    part = pl.program_id(0)
    me = lax.axis_index("ctx")

    def block_of(slot):
        low = order_ref[slot // 2]
        return low if slot % 2 == 0 else 2 * n_ctx - 1 - low

    @pl.when(part == 0)
    def _():
        copies = []
        for slot in range(2 * n_ctx):
            first = pl.multiple_of(block_of(slot) * half, half)
            copy = pltpu.make_async_copy(
                lat_ref.at[pl.ds(slot * half, half)], keys.at[pl.ds(first, half)], sems.at[slot]
            )
            copy.start()
            copies.append(copy)
        keys[pl.ds(seq, KEY_TILE)] = jnp.zeros((KEY_TILE, keys.shape[1]), keys.dtype)
        grad_keys[...] = jnp.zeros_like(grad_keys)
        bounds[0] = 0
        for number in range(1, DOCS):
            at = jnp.int32(0)
            step = seq // 2
            while step >= 1:
                at = jnp.where(docs_ref[at + step - 1] < number, at + step, at)
                step //= 2
            bounds[number] = at
        for copy in copies:
            copy.wait()

    low = order_ref[me]
    pos0 = jnp.where(part == 0, low, 2 * n_ctx - 1 - low) * half
    doc_start = jnp.int32(0)
    for number in range(1, DOCS):
        doc_start = jnp.where(bounds[number] <= pos0, bounds[number], doc_start)
    start = (doc_start // 16) * 16
    tiles = (pos0 + half - start + KEY_TILE - 1) // KEY_TILE

    row_pos = pos0 + lax.rem(lax.broadcasted_iota(jnp.int32, (1, cols), 1), half)
    row_doc = jnp.zeros_like(row_pos)
    for number in range(1, DOCS):
        row_doc = jnp.where(bounds[number] <= row_pos, bounds[number], row_doc)

    def tile_at(i):
        return pl.ds(pl.multiple_of(start + i * KEY_TILE, 16), KEY_TILE)

    heads_now = cols // half
    for chunk in range(heads * half // cols):
        here = slice(chunk * cols, (chunk + 1) * cols)

        def first_pass(i, row_max):
            at = tile_at(i)
            s = dot(keys[at, :], q_ref[0, :, here], NN) * score_scale
            key_pos = start + i * KEY_TILE + lax.broadcasted_iota(jnp.int32, (KEY_TILE, 1), 0)
            s = jnp.where((key_pos <= row_pos) & (key_pos >= row_doc), s, far_below)
            scores[i] = s
            grad_probs[i] = dot(keys[at, :lat], g_ref[0, here, :], NT)
            return jnp.maximum(row_max, jnp.max(s, axis=0, keepdims=True))

        row_max = lax.fori_loop(
            0, tiles, first_pass, jnp.full((1, cols), far_below, jnp.float32)
        )

        def second_pass(i, sums):
            row_sum, weighted = sums
            e = jnp.exp(scores[i] - row_max)
            scores[i] = e
            return (
                row_sum + jnp.sum(e, axis=0, keepdims=True),
                weighted + jnp.sum(e * grad_probs[i], axis=0, keepdims=True),
            )

        zero = jnp.zeros((1, cols), jnp.float32)
        row_sum, weighted = lax.fori_loop(0, tiles, second_pass, (zero, zero))
        inverse = 1.0 / row_sum
        delta = weighted * inverse
        scaled = inverse * score_scale

        def third_pass(i, first):
            at = tile_at(i)
            e = scores[i]
            probs = (e * inverse).astype(jnp.bfloat16)
            ds = (e * scaled * (grad_probs[i] - delta)).astype(jnp.bfloat16)
            out_now = dot(probs, keys[at, :lat], TN)
            q_now = dot(keys[at, :], ds, TN)
            out_acc[...] = out_now if first else out_acc[...] + out_now
            q_acc[...] = q_now if first else q_acc[...] + q_now
            key_term = dot(ds, q_ref[0, :, here], NT)
            value_term = dot(probs, g_ref[0, here, :], NN)
            grad_keys[at, :lat] += key_term[:, :lat] + value_term
            grad_keys[at, lat:] += key_term[:, lat:]

        third_pass(0, True)

        @pl.loop(1, tiles)
        def _(i):
            third_pass(i, False)

        for k in range(heads_now):
            head = chunk * heads_now + k
            mine = slice(k * half, (k + 1) * half)
            for lanes in range(lat // LANES):
                by_token[lanes, pl.ds(head, half, stride=heads), :] = out_acc[
                    mine, lanes * LANES : (lanes + 1) * LANES
                ]

        for p in range(2):
            @pl.when(part == p)
            def _():
                for k in range(heads_now):
                    head = chunk * heads_now + k
                    mine = slice(k * half, (k + 1) * half)
                    gq_ref[head, :, p * half : (p + 1) * half] = q_acc[:, mine].astype(
                        gq_ref.dtype
                    )

    for lanes in range(lat // LANES):
        out_ref[:, lanes * LANES : (lanes + 1) * LANES] = by_token[lanes].astype(out_ref.dtype)

    @pl.when(part == 1)
    def _():
        for slot in range(2 * n_ctx):
            first = pl.multiple_of(block_of(slot) * half, half)
            gl_ref[pl.ds(slot * half, half), :] = grad_keys[pl.ds(first, half), :].astype(
                gl_ref.dtype
            )


def attention(q_cols, g_rows, all_lat, block_order, doc_ids, n_ctx, heads):
    width, total = q_cols.shape[1:]
    lat = g_rows.shape[2]
    half = total // heads
    tok = 2 * half
    seq = tok * n_ctx
    cols = min(total, COLS)
    tile_count = seq // KEY_TILE + 1
    return pl.pallas_call(
        functools.partial(attention_kernel, (n_ctx, half, heads, cols, lat)),
        grid_spec=pltpu.PrefetchScalarGridSpec(
            num_scalar_prefetch=2,
            grid=(2,),
            in_specs=[
                pl.BlockSpec((1, width, total), lambda p, *_: (p, 0, 0)),
                pl.BlockSpec((1, total, lat), lambda p, *_: (p, 0, 0)),
                pl.BlockSpec(memory_space=pl.ANY),
            ],
            out_specs=[
                pl.BlockSpec((total, lat), lambda p, *_: (p, 0)),
                pl.BlockSpec((heads, width, tok), lambda p, *_: (0, 0, 0)),
                pl.BlockSpec((seq, width), lambda p, *_: (0, 0)),
            ],
            scratch_shapes=[
                pltpu.VMEM((seq + KEY_TILE, width), jnp.bfloat16),
                pltpu.VMEM((seq + KEY_TILE, width), jnp.float32),
                pltpu.VMEM((tile_count, KEY_TILE, cols), jnp.float32),
                pltpu.VMEM((tile_count, KEY_TILE, cols), jnp.float32),
                pltpu.VMEM((cols, lat), jnp.float32),
                pltpu.VMEM((width, cols), jnp.float32),
                pltpu.VMEM((lat // LANES, total, LANES), jnp.float32),
                pltpu.SMEM((DOCS,), jnp.int32),
                pltpu.SemaphoreType.DMA((2 * n_ctx,)),
            ],
        ),
        out_shape=[
            jax.ShapeDtypeStruct((tok * heads, lat), jnp.bfloat16),
            jax.ShapeDtypeStruct((heads, width, tok), jnp.bfloat16),
            jax.ShapeDtypeStruct((seq, width), jnp.bfloat16),
        ],
        compiler_params=pltpu.CompilerParams(vmem_limit_bytes=56 * 1024 * 1024),
        cost_estimate=pl.CostEstimate(
            flops=14 * tok * heads * seq * lat // 2, bytes_accessed=12 << 20, transcendentals=0
        ),
    )(block_order, doc_ids, q_cols, g_rows, all_lat)


def transfer(src, dst, sems, index, device):
    copy = pltpu.make_async_remote_copy(
        src_ref=src, dst_ref=dst, send_sem=sems.at[0, index], recv_sem=sems.at[1, index],
        device_id=device, device_id_type=pl.DeviceIdType.MESH,
    )
    copy.start()
    return copy


def greet(peers):
    barrier = pltpu.get_barrier_semaphore()
    for peer in peers:
        pl.semaphore_signal(
            barrier, inc=1, device_id=peer, device_id_type=pl.DeviceIdType.MESH
        )
    pl.semaphore_wait(barrier, len(peers))


def places(n_ctx):
    me = lax.axis_index("ctx")
    core = lax.rem(me, 2)
    chip = me // 2
    sibling = chip * 2 + 1 - core
    chips = n_ctx // 2
    return me, core, chip, sibling, chips


def gather_kernel(
    n_ctx, lat_ref, q_hbm, g_hbm, out_ref, q_hbm_out, g_hbm_out, own, q_in, g_in, q_out,
    g_out, g_wide,
    sems, pair_sems, local_sems,
):
    me, core, chip, sibling, chips = places(n_ctx)
    z = lax.axis_index("head")
    others = [lax.rem(chip + k, chips) * 2 + core for k in range(1, chips)]
    loads = [
        pltpu.make_async_copy(q_hbm, q_in, local_sems.at[0]),
        pltpu.make_async_copy(g_hbm, g_in, local_sems.at[1]),
    ]
    for load in loads:
        load.start()
    own[...] = lat_ref[...].T
    greet([(sibling, z)] + [(other, z) for other in others])
    sends = [
        transfer(own, out_ref.at[me], sems, k, (other, z)) for k, other in enumerate(others)
    ]
    pairs = [transfer(own, out_ref.at[me], pair_sems, 0, (sibling, z))]
    keep = pltpu.make_async_copy(own, out_ref.at[me], local_sems.at[2])
    keep.start()

    heads, width, tok = q_in.shape
    half = tok // 2
    loads[0].wait()

    def pack_heads(k, carry):
        a, b = q_in[2 * k], q_in[2 * k + 1]
        at = pl.ds(pl.multiple_of(k * tok, tok), tok)
        q_out[0, :, at] = jnp.concatenate([a[:, :half], b[:, :half]], axis=1)
        q_out[1, :, at] = jnp.concatenate([a[:, half:], b[:, half:]], axis=1)
        return carry

    lax.fori_loop(0, heads // 2, pack_heads, 0)
    stores = [
        pltpu.make_async_copy(q_out, q_hbm_out, local_sems.at[3]),
        pltpu.make_async_copy(g_out, g_hbm_out, local_sems.at[4]),
    ]
    stores[0].start()
    loads[1].wait()
    for p in range(2):
        for lanes in range(g_wide.shape[0]):
            at = slice(lanes * LANES, (lanes + 1) * LANES)
            g_wide[lanes] = g_in[p * half * heads : (p + 1) * half * heads, at].astype(jnp.float32)
            for head in range(heads):
                g_out[p, head * half : (head + 1) * half, at] = g_wide[
                    lanes, pl.ds(head, half, stride=heads), :
                ].astype(g_out.dtype)

    stores[1].start()
    for k in range(1, chips):
        sends[k - 1].wait_recv()
        owner = lax.rem(chip + chips - k, chips) * 2 + core
        pairs.append(
            transfer(out_ref.at[owner], out_ref.at[owner], pair_sems, k, (sibling, z))
        )
    for copy in sends:
        copy.wait_send()
    for copy in pairs:
        copy.wait()
    for copy in stores:
        copy.wait()
    keep.wait()


def gather(latents, queries, grad_out, n_ctx):
    tok, width = latents.shape
    heads, lat = grad_out.shape[1:]
    total = heads * tok // 2
    vmem = pl.BlockSpec(memory_space=pltpu.VMEM)
    hbm = pl.BlockSpec(memory_space=pl.ANY)
    kind = latents.dtype
    out, q_cols, g_rows = pl.pallas_call(
        functools.partial(gather_kernel, n_ctx),
        in_specs=[vmem, hbm, hbm],
        out_specs=[hbm, hbm, hbm],
        out_shape=[
            jax.ShapeDtypeStruct((n_ctx, tok, width), kind),
            jax.ShapeDtypeStruct((2, width, total), kind),
            jax.ShapeDtypeStruct((2, total, lat), kind),
        ],
        scratch_shapes=[
            pltpu.VMEM((tok, width), kind),
            pltpu.VMEM((heads, width, tok), kind),
            pltpu.VMEM((tok * heads, lat), kind),
            pltpu.VMEM((2, width, total), kind),
            pltpu.VMEM((2, total, lat), kind),
            pltpu.VMEM((lat // LANES, total, LANES), jnp.float32),
            pltpu.SemaphoreType.DMA((2, n_ctx // 2)),
            pltpu.SemaphoreType.DMA((2, n_ctx // 2)),
            pltpu.SemaphoreType.DMA((5,)),
        ],
        compiler_params=pltpu.CompilerParams(
            collective_id=0, has_side_effects=True, vmem_limit_bytes=56 * 1024 * 1024
        ),
    )(latents.T, jnp.transpose(queries, (1, 2, 0)), grad_out.reshape(tok * heads, lat))
    return out.reshape(n_ctx * tok, width), q_cols, g_rows


def reduce_kernel(
    n_ctx, n_head, part_ref, out_ref, pair_in, chip_out, chip_in, head_out, head_in, whole, sum_own,
    mine, load_sems,
    pair_sems, chip_sems, head_sems, last_sems,
):
    me, core, chip, sibling, chips = places(n_ctx)
    z = lax.axis_index("head")
    others = [lax.rem(chip + k, chips) * 2 + core for k in range(1, chips)]
    heads = [lax.rem(z + k, n_head) for k in range(1, n_head)]
    order = [lax.rem(chip + k, chips) for k in range(1, chips + 1)]
    loads = [
        pltpu.make_async_copy(part_ref.at[target * 2 + core], mine.at[k], load_sems.at[k])
        for k, target in enumerate(order)
    ]
    for load in loads:
        load.start()
    greet(
        [(sibling, z)] + [(other, z) for other in others] + [(me, other) for other in heads]
    )
    parts = part_ref.shape[1]
    rows = part_ref.shape[2] // n_head
    pairs = [
        [
            transfer(
                part_ref.at[target * 2 + 1 - core, s], pair_in.at[s, k], pair_sems.at[s], k,
                (sibling, z),
            )
            for k, target in enumerate(order)
        ]
        for s in range(parts)
    ]
    for load in loads:
        load.wait()
    sends, steps, lasts = [], [], []
    for s in range(parts):
        sent = []
        for k, target in enumerate(order):
            pairs[s][k].wait_recv()
            total = mine[k, s].astype(jnp.float32) + pair_in[s, k].astype(jnp.float32)
            if k < chips - 1:
                chip_out[s, k] = total.astype(jnp.bfloat16)
                sent.append(
                    transfer(
                        chip_out.at[s, k], chip_in.at[s, k], chip_sems.at[s], k, (others[k], z)
                    )
                )
        sum_own[s] = total
        sends.append(sent)
    for s in range(parts):
        total = sum_own[s]
        for k, copy in enumerate(sends[s]):
            copy.wait_recv()
            total = total + chip_in[s, k].astype(jnp.float32)
        for k in range(n_head):
            head_out[s, k] = total[k * rows : (k + 1) * rows].astype(jnp.bfloat16)
        steps.append([
            transfer(head_out.at[s, other], head_in.at[s, k], head_sems.at[s], k, (me, other))
            for k, other in enumerate(heads)
        ])
    for s in range(parts):
        piece = head_out[s, z].astype(jnp.float32)
        for k, copy in enumerate(steps[s]):
            copy.wait_recv()
            piece = piece + head_in[s, k].astype(jnp.float32)
        whole[s, z] = piece.astype(jnp.bfloat16)
        lasts.append([
            transfer(whole.at[s, z], whole.at[s, z], last_sems.at[s], k, (me, other))
            for k, other in enumerate(heads)
        ])
    for copies in lasts:
        for copy in copies:
            copy.wait_recv()
    result = jnp.concatenate(
        [whole[s, k] for s in range(parts) for k in range(n_head)], axis=0
    )
    out_ref[...] = result.astype(jnp.float32).T
    for copies in pairs + sends + steps + lasts:
        for copy in copies:
            copy.wait_send()


def reduce_parts(parts, n_ctx, n_head):
    seq, width = parts.shape
    tok = seq // n_ctx
    splits = 2 if tok // (2 * n_head) >= 16 else 1
    deep = tok // splits
    rows = deep // n_head
    chips = n_ctx // 2
    kind = parts.dtype
    vmem = pl.BlockSpec(memory_space=pltpu.VMEM)
    out = pl.pallas_call(
        functools.partial(reduce_kernel, n_ctx, n_head),
        in_specs=[pl.BlockSpec(memory_space=pl.ANY)],
        out_specs=vmem,
        out_shape=jax.ShapeDtypeStruct((width, tok), jnp.float32),
        scratch_shapes=[
            pltpu.VMEM((splits, chips, deep, width), kind),
            pltpu.VMEM((splits, chips, deep, width), kind),
            pltpu.VMEM((splits, chips, deep, width), kind),
            pltpu.VMEM((splits, n_head, rows, width), kind),
            pltpu.VMEM((splits, n_head, rows, width), kind),
            pltpu.VMEM((splits, n_head, rows, width), kind),
            pltpu.VMEM((splits, deep, width), jnp.float32),
            pltpu.VMEM((chips, splits, deep, width), kind),
            pltpu.SemaphoreType.DMA((chips,)),
            pltpu.SemaphoreType.DMA((splits, 2, chips)),
            pltpu.SemaphoreType.DMA((splits, 2, chips)),
            pltpu.SemaphoreType.DMA((splits, 2, n_head)),
            pltpu.SemaphoreType.DMA((splits, 2, n_head)),
        ],
        compiler_params=pltpu.CompilerParams(
            collective_id=1, has_side_effects=True, vmem_limit_bytes=56 * 1024 * 1024
        ),
    )(parts.reshape(n_ctx, splits, deep, width))
    return out.T


def body(queries, latents, grad_out, block_order, doc_ids):
    n_ctx = lax.axis_size("ctx")
    n_head = lax.axis_size("head")
    tok, heads, lat = grad_out.shape
    all_lat, q_cols, g_rows = gather(latents, queries, grad_out, n_ctx)
    out, gq, gl = attention(q_cols, g_rows, all_lat, block_order, doc_ids, n_ctx, heads)
    grad_latents = reduce_parts(gl, n_ctx, n_head)
    return out.reshape(tok, heads, lat), jnp.transpose(gq, (2, 0, 1)), grad_latents


def solution(mesh):
    return jax.shard_map(
        body,
        mesh=mesh,
        in_specs=(P("ctx", "head", None), P("ctx", None), P("ctx", "head", None), P(), P()),
        out_specs=(P("ctx", "head", None), P("ctx", "head", None), P("ctx", None)),
        check_vma=False,
    )
```
